256 devices in a mesh: ma: 2 (over core), ta: 128 (over y, x, z).
Axes of the slice: x: 4, y: 4, z: 8, core: 2. Of those that a mesh axis runs over, the one named last changes fastest.
Arguments:
- thickness: float32 [512, 128, 128], P('ta'), may hold values from 0.5 to 2
- driving: float32 [2, 512, 128, 128], P(None, 'ta'), may hold values from -6 to 6
- friction: float32 [1024, 128, 128], P(('ma', 'ta')), parts along dimension 0, may hold values from 0.3 to 3
- velocity_start: float32 [2, 512, 128, 128], P(None, 'ta'), may hold values from -6 to 6
- row_lengths: int32 [22], replicated, may hold values from 1 to 48, 512 in all
Outputs:
- velocity: float32 [2, 1024, 128, 128], P(None, ('ma', 'ta')), parts along dimension 1
- thickness_next: float32 [1024, 128, 128], P(('ma', 'ta')), parts along dimension 0
The draws below stay inside these ranges and needn't reach their ends.
There are 2 independent parts, one for each index of `ma`. The reference program is written for one: setup_inputs(seed, part) draws one part's arguments, and reference() takes and returns one part's arrays. A program takes and returns all parts, laid end to end along the dimension named above; an argument that names none is the same for every part. Nothing has to cross between parts.
Inputs may be any that keep to these rules, and one draw needn't show every extreme that they name: Tile row r is ice in its last row_lengths[r] of 48 tile columns; the lengths sum to 512, and at least one row is ice in all 48 columns.
All inputs are finite; a program needn't handle non-finite values.
Results may differ from the reference program's by a relative error of at most 0.0003.
Values sent between devices are 32-bit elements; how exact they have to be, the bound alone decides.
No kernel may reach another device: no remote copies, remote signals or barrier semaphores. Data moves between devices by JAX's collectives and lax.ppermute only.
A program may use at most 128 MiB of HBM per device.

```python
import math
import jax
import jax.numpy as jnp
import numpy as np

TS = 128
GC = 48
SWEEPS = 4
TILES = 512
GR = 22


def steps_of(rng, shape, pieces, smallest, top_value):
    loudness = 1.0
    for dim, blocks in pieces:
        steps = jax.random.uniform(jax.random.fold_in(jax.random.fold_in(rng, 6), dim), (blocks,), jnp.float32, smallest / len(pieces), top_value / len(pieces))
        loudness = loudness * jnp.repeat(jnp.exp(steps), shape[dim] // blocks).reshape((-1,) + (1,) * (len(shape) - 1 - dim))
    return loudness


def split_up(count, total, bound, lean):
    weights = [(1 << 20) // math.isqrt(grade ** lean) + 1 for grade in range(2, count + 1)]
    surplus, holding = total - bound - (count - 1), [1] * (count - 1)
    while surplus > 0:
        free = [i for i in range(count - 1) if holding[i] < bound]
        mass, left = sum([weights[i] for i in free]), surplus
        for i in free:
            addition = min(bound - holding[i], max(1, left * weights[i] // mass), surplus)
            holding[i] = holding[i] + addition
            surplus = surplus - addition
    return np.array([bound] + holding)


def uneven(own_key, count, total, limit, skew):
    if count == 2:
        one = jax.random.randint(own_key, (), max(1, total - limit), min(limit, total - 1) + 1)
        return jnp.stack([one, total - one])
    sizes = jnp.asarray(split_up(count, total, limit, skew), jnp.int32)
    pairs = (count - 1) // 2
    donor, taker = sizes[1:1 + 2 * pairs:2], sizes[2:2 + 2 * pairs:2]
    slack = jnp.minimum(donor - 1, limit - taker)
    passed = jax.random.randint(jax.random.fold_in(own_key, 1), (pairs,), 0, 1 << 20) % (slack + 1)
    sizes = sizes.at[1:1 + 2 * pairs:2].set(donor - passed).at[2:2 + 2 * pairs:2].set(taker + passed)
    return sizes[jax.random.permutation(jax.random.fold_in(own_key, 2), count)]


def noise(stream_key, extent, width, most, cuts=(), held_as=jnp.bfloat16):
    factor_of = steps_of(stream_key, extent, cuts, -0.22, 0.18) if cuts else 1.0
    entries = jax.random.normal(stream_key, extent, jnp.float32) * width * factor_of
    return jnp.minimum(jnp.maximum(entries, -most), most).astype(held_as)


def setup_inputs(seed: int = 0, part: int = 0) -> dict:
    keys = jax.random.split(jax.random.key(seed), 6)
    part_splits = jax.random.split(jax.random.fold_in(keys[5], part), 6)
    return {
        "thickness": jnp.clip(0.5 + 1.5 * jax.random.uniform(keys[0], (TILES, TS, TS), jnp.float32) ** steps_of(keys[0], (TILES, TS, TS), ((0, 128),), -0.2, 0.2), 0.5, 2.0),
        "driving": noise(keys[1], (2, TILES, TS, TS), 1.0, 6.0, ((1, 128),), jnp.float32),
        "friction": jnp.clip(jnp.exp(math.log(3.0) - 2.3025851 * jax.random.uniform(part_splits[2], (TILES, TS, TS), jnp.float32) ** steps_of(part_splits[2], (TILES, TS, TS), ((0, 128),), -0.2, 0.2)), 0.3, 3.0),
        "velocity_start": noise(keys[3], (2, TILES, TS, TS), 1.0, 6.0, ((1, 128),), jnp.float32),
        "row_lengths": uneven(keys[4], GR, TILES, GC, 1).astype(jnp.int32),
    }


STRAIN_EPSILON = 0.01
TIME_STEP = 0.1


def tile_neighbours(row_lengths, tile_slots):
    lengths = row_lengths.astype(jnp.int32)
    row_ends = jnp.cumsum(lengths).astype(jnp.int32)
    row_ids = jnp.arange(lengths.shape[0], dtype=jnp.int32)
    tile_row = jnp.sum((row_ends[None, :] <= tile_slots[:, None]).astype(jnp.int32), axis=1).astype(jnp.int32)

    def lookup(values_table, wanted):
        hits = jnp.where(row_ids[None, :] == wanted[:, None], values_table[None, :], 0)
        return jnp.sum(hits, axis=1).astype(jnp.int32)

    this_len = lookup(lengths, tile_row)
    this_end = lookup(row_ends, tile_row)
    above_len = lookup(lengths, tile_row - 1)
    below_len = lookup(lengths, tile_row + 1)
    column = GC + tile_slots - this_end
    missing = jnp.full_like(tile_slots, -1)
    lower_y = jnp.where(column >= GC - above_len, tile_slots - this_len, missing)
    upper_y = jnp.where(column >= GC - below_len, tile_slots + below_len, missing)
    lower_x = jnp.where(column - 1 >= GC - this_len, tile_slots - 1, missing)
    upper_x = jnp.where(column + 1 < GC, tile_slots + 1, missing)
    return jnp.stack([lower_y, upper_y, lower_x, upper_x], axis=1).astype(jnp.int32)


def facing_edges(fields):
    return jnp.stack([fields[:, :, -1, :], fields[:, :, 0, :], fields[:, :, :, -1], fields[:, :, :, 0]], axis=2)


def pick_edges(source, index, present):
    edge_ids = jnp.arange(index.shape[1], dtype=jnp.int32)[None, :]
    values = source[:, index, edge_ids, :]
    return jnp.where(present[None, :, :, None], values, 0.0)


def neighbour_views(fields, edges):
    lower_y = jnp.concatenate([edges[:, :, 0, None, :], fields[:, :, :-1, :]], axis=2)
    upper_y = jnp.concatenate([fields[:, :, 1:, :], edges[:, :, 1, None, :]], axis=2)
    lower_x = jnp.concatenate([edges[:, :, 2, :, None], fields[:, :, :, :-1]], axis=3)
    upper_x = jnp.concatenate([fields[:, :, :, 1:], edges[:, :, 3, :, None]], axis=3)
    return lower_y, upper_y, lower_x, upper_x


def viscosity_of(beside_all, thickness):
    lower_y, upper_y, lower_x, upper_x = beside_all
    strain_xx = 0.5 * (upper_x[0] - lower_x[0])
    shear_uy = 0.5 * (upper_y[0] - lower_y[0])
    shear_vx = 0.5 * (upper_x[1] - lower_x[1])
    strain_yy = 0.5 * (upper_y[1] - lower_y[1])
    shear_sum = shear_uy + shear_vx
    strain = strain_xx * strain_xx + strain_yy * strain_yy + strain_xx * strain_yy + 0.25 * shear_sum * shear_sum + STRAIN_EPSILON
    return thickness * 0.5 * jnp.power(strain, -1.0 / 3.0)


def relax(beside_all, viscosity, viscosity_around, friction, driving):
    lower_y, upper_y, lower_x, upper_x = beside_all
    coef_ly = 0.5 * (viscosity + viscosity_around[0][0])
    coef_uy = 0.5 * (viscosity + viscosity_around[1][0])
    coef_lx = 0.5 * (viscosity + viscosity_around[2][0])
    coef_ux = 0.5 * (viscosity + viscosity_around[3][0])
    u_top = 4.0 * (coef_lx * lower_x[0] + coef_ux * upper_x[0]) + coef_ly * lower_y[0] + coef_uy * upper_y[0] - driving[0]
    u_bottom = 4.0 * (coef_lx + coef_ux) + coef_ly + coef_uy + friction
    v_top = coef_lx * lower_x[1] + coef_ux * upper_x[1] + 4.0 * (coef_ly * lower_y[1] + coef_uy * upper_y[1]) - driving[1]
    v_bottom = coef_lx + coef_ux + 4.0 * (coef_ly + coef_uy) + friction
    return jnp.stack([u_top / u_bottom, v_top / v_bottom])


def transport(velocity, thickness, beside_all):
    lower_y, upper_y, lower_x, upper_x = beside_all
    speed_lx = 0.5 * (lower_x[0] + velocity[0])
    speed_ux = 0.5 * (velocity[0] + upper_x[0])
    speed_ly = 0.5 * (lower_y[1] + velocity[1])
    speed_uy = 0.5 * (velocity[1] + upper_y[1])
    flux_lx = jnp.maximum(speed_lx, 0.0) * lower_x[2] + jnp.minimum(speed_lx, 0.0) * thickness
    flux_ux = jnp.maximum(speed_ux, 0.0) * thickness + jnp.minimum(speed_ux, 0.0) * upper_x[2]
    flux_ly = jnp.maximum(speed_ly, 0.0) * lower_y[2] + jnp.minimum(speed_ly, 0.0) * thickness
    flux_uy = jnp.maximum(speed_uy, 0.0) * thickness + jnp.minimum(speed_uy, 0.0) * upper_y[2]
    return thickness - TIME_STEP * (flux_ux - flux_lx + flux_uy - flux_ly)


def reference(thickness, driving, friction, velocity_start, row_lengths):
    tile_slots = jnp.arange(thickness.shape[0], dtype=jnp.int32)
    neighbour = tile_neighbours(row_lengths, tile_slots)
    present = neighbour >= 0
    source_slot = jnp.maximum(neighbour, 0).astype(jnp.int32)

    def edge_halo(fields):
        return pick_edges(facing_edges(fields), source_slot, present)

    velocity = velocity_start
    for sweep in range(SWEEPS):
        beside_all = neighbour_views(velocity, edge_halo(velocity))
        viscosity = viscosity_of(beside_all, thickness)
        viscosity_fields = viscosity[None]
        viscosity_around = neighbour_views(viscosity_fields, edge_halo(viscosity_fields))
        velocity = relax(beside_all, viscosity, viscosity_around, friction, driving)
    carried = jnp.concatenate([velocity, thickness[None]], axis=0)
    beside_all = neighbour_views(carried, edge_halo(carried))
    thickness_next = transport(velocity, thickness, beside_all)
    return velocity, thickness_next
```

```python
import functools

import jax
import jax.numpy as jnp
from jax import lax
from jax.experimental import pallas as pl
from jax.experimental.pallas import tpu as pltpu
from jax.sharding import PartitionSpec as P


GC = 48
SWEEPS = 4
STRAIN_EPSILON = 0.01
TIME_STEP = 0.1

TS = 128
LANES = 128
TPD = 4
SECTION = 8
STRIP = 6 * SECTION
TOP = 16
ROWS = TS + 2 * TOP
MARGIN = 16
STRIDE = 3
HOPS = 5
MAIN_BLOCKS = 2 * TPD
PACK = (MAIN_BLOCKS + 2) * STRIP
FULL_PACK = PACK + TS
VMEM_LIMIT = 40 * 1024 * 1024


def cyclic_shift(value, steps):
    count = lax.axis_size("ta")
    return lax.ppermute(value, "ta", [(i, (i + steps) % count) for i in range(count)])


def fill_row_ends(len_ref, ends_ref):
    total = jnp.int32(0)
    ends = []
    for r in range(len_ref.shape[0]):
        total = total + len_ref[r]
        ends_ref[r] = total
        ends.append(total)
    return ends


class Tile:
    def __init__(self, len_ref, ends_ref, ends, slot, slots):
        rows = len_ref.shape[0]
        row = jnp.int32(0)
        for end in ends:
            row = row + jnp.where(end <= slot, 1, 0)
        self.slot = slot
        self.real = (slot >= 0) & (slot < slots)
        row = jnp.minimum(row, rows - 1)
        self.length = len_ref[row]
        self.above = jnp.where(row >= 1, len_ref[jnp.maximum(row - 1, 0)], 0)
        self.below = jnp.where(row < rows - 1, len_ref[jnp.minimum(row + 1, rows - 1)], 0)
        self.column = GC + slot - ends_ref[row]

    def side(self, down, step):
        column = self.column + step
        length = self.below if down else self.above
        there = self.real & (column < GC) & (column >= GC - length)
        slot = self.slot + (self.below if down else -self.length) + step
        return there, slot

    def lower_x(self):
        return self.real & (self.column > GC - self.length)

    def upper_x(self):
        return self.real & (self.column < GC - 1)


def hop(device, slot, down):
    owner = slot >> 2
    q = jnp.maximum((owner - device) if down else (device - owner), 0)
    a = jnp.minimum(((q + 1) * 11) >> 5, HOPS - 1)
    b = q - STRIDE * a
    return a, (-b if down else b)


def strips_kernel(h_ref, d_ref, f_ref, v_ref, bottom_ref, top_ref, right_ref, left_ref):
    fields = [v_ref.at[0], v_ref.at[1], h_ref, d_ref.at[0], d_ref.at[1], f_ref]
    row = lax.broadcasted_iota(jnp.int32, (SECTION, LANES), 0)
    lane = lax.broadcasted_iota(jnp.int32, (TS, LANES), 1)
    for t in range(TPD):
        for k, field in enumerate(fields):
            last = field[t, TS - SECTION :, :]
            first = field[t, :SECTION, :]
            if k in (3, 4):
                extra = fields[k - 3]
                last = jnp.where(row == 0, extra[t, TS - SECTION - 1 : TS - SECTION, :], last)
                first = jnp.where(row == SECTION - 1, extra[t, SECTION : SECTION + 1, :], first)
            bottom_ref[t, k * SECTION : (k + 1) * SECTION, :] = last
            top_ref[t, k * SECTION : (k + 1) * SECTION, :] = first
    right = jnp.zeros((TS, LANES), jnp.float32)
    left = jnp.zeros((TS, LANES), jnp.float32)
    for k, field in enumerate(fields):
        here = (lane >> 4) == k
        right = jnp.where(here, pltpu.roll(field[TPD - 1], (MARGIN * k + MARGIN) % LANES, 1), right)
        left = jnp.where(here, pltpu.roll(field[0], MARGIN * k, 1) if k else field[0], left)
    right_ref[...] = right
    left_ref[...] = left


def route_kernel(slots, len_ref, *refs):
    given = refs[: 2 * HOPS]
    right_ref, left_ref = refs[2 * HOPS : 2 * HOPS + 2]
    outs = refs[2 * HOPS + 2 : 2 * HOPS + 5]
    strips, ends_ref, sems = refs[2 * HOPS + 5 :]
    copies = [
        pltpu.make_async_copy(given[i], strips.at[i // HOPS, i % HOPS], sems.at[i]) for i in range(2 * HOPS)
    ]
    for copy in copies:
        copy.start()
    ends = fill_row_ends(len_ref, ends_ref)
    outs[0][PACK:, :] = left_ref[...]
    outs[2][PACK:, :] = right_ref[...]
    for out in outs:
        out[MAIN_BLOCKS * STRIP : PACK, :] = jnp.zeros((2 * STRIP, LANES), jnp.float32)
    lane = lax.broadcasted_iota(jnp.int32, (STRIP, LANES), 1)
    me, count = lax.axis_index("ta"), slots // TPD
    for copy in copies:
        copy.wait()
    for step, out in zip((-1, 0, 1), outs):
        device = lax.rem(me + step + count, count)
        for j in range(TPD):
            tile = Tile(len_ref, ends_ref, ends, device * TPD + j, slots)
            for down in (0, 1):
                for across in (-1, 0, 1):
                    there, slot = tile.side(down, across)
                    a, shift = hop(device, slot, down)

                    @pl.when(there & (shift == step))
                    def _(out=out, j=j, down=down, across=across, a=a, slot=slot):
                        strip = strips[down, a, slot & 3]
                        if across == 0:
                            block = down * TPD + j
                            out[block * STRIP : (block + 1) * STRIP, :] = strip
                        else:
                            block = MAIN_BLOCKS + down
                            first = 2 * j + (across + 1) // 2
                            moved = pltpu.roll(strip, (2 * MARGIN * j + MARGIN) % LANES, 1)
                            rows = slice(block * STRIP, (block + 1) * STRIP)
                            out[rows, :] = jnp.where((lane >> 4) == first, moved, out[rows, :])


def group_mask(flags, shape):
    bits = jnp.int32(0)
    for k, flag in enumerate(flags):
        bits = bits + jnp.where(flag, 1 << k, 0)
    group = lax.broadcasted_iota(jnp.int32, shape, 1) >> 4
    return ((jnp.full(shape, bits) >> group) & 1) == 1


def sweeps_kernel(
    slots, len_ref, h_ref, d_ref, f_ref, v_ref, back_ref, local_ref, ahead_ref,
    vel_ref, next_ref, u, v, w, h, d0, d1, f, ice, packs, ends_ref, sems,
):
    own = (pl.ds(0, TPD), pl.ds(TOP, TS))
    copies = [
        (v_ref.at[0], u.at[(0,) + own]),
        (v_ref.at[1], v.at[(0,) + own]),
        (h_ref, h.at[own]),
        (d_ref.at[0], d0.at[own]),
        (d_ref.at[1], d1.at[own]),
        (f_ref, f.at[own]),
        (back_ref, packs.at[0]),
        (local_ref, packs.at[1, pl.ds(0, PACK)]),
        (ahead_ref, packs.at[2]),
    ]
    copies = [pltpu.make_async_copy(a, b, sems.at[i]) for i, (a, b) in enumerate(copies)]
    for copy in copies:
        copy.start()
    me = lax.axis_index("ta")
    ends = fill_row_ends(len_ref, ends_ref)
    tiles = [Tile(len_ref, ends_ref, ends, me * TPD + j, slots) for j in range(TPD)]
    zero = jnp.zeros((SECTION, LANES), jnp.float32)
    one = jnp.ones((SECTION, LANES), jnp.float32)
    for block in range(TPD + 1):
        for start in (0, ROWS - SECTION):
            rows = slice(start, start + SECTION)
            u[0, block, rows, :] = zero
            v[0, block, rows, :] = zero
            w[block, rows, :] = zero
    for copy in copies:
        copy.wait()

    targets = (u.at[0], v.at[0], h, d0, d1, f)
    for down in (0, 1):
        start = TOP + TS if down else TOP - SECTION
        rows = slice(start, start + SECTION)
        deep = SECTION - 1 if down else 0
        far = start + SECTION if down else start - 1
        for j in range(TPD + 1):
            if j < TPD:
                there, slot = tiles[j].side(down, 0)
                _, shift = hop(me, slot, down)
                which = jnp.where(there, shift + 1, 1)
                base = (down * TPD + j) * STRIP
                parts = [packs[which, base + k * SECTION : base + (k + 1) * SECTION, :] for k in range(6)]
                mask = jnp.full((SECTION, LANES), jnp.where(there, 1, 0)) == 1
            else:
                base = (MAIN_BLOCKS + down) * STRIP
                parts = [
                    packs[0, base + k * SECTION : base + (k + 1) * SECTION, :]
                    + packs[1, base + k * SECTION : base + (k + 1) * SECTION, :]
                    + packs[2, base + k * SECTION : base + (k + 1) * SECTION, :]
                    for k in range(6)
                ]
                flags = [tile.side(down, across)[0] for tile in tiles for across in (-1, 1)]
                mask = group_mask(flags, (SECTION, LANES))
            for k, target in enumerate(targets):
                target[j, rows, :] = jnp.where(mask, parts[k], one if k == 5 else zero)
            for k in (0, 1):
                line = jnp.where(mask, parts[3 + k], zero)
                targets[k][j, far : far + 1, :] = line[deep : deep + 1, :]
            ice[j, rows, :] = jnp.where(mask, one, zero)

    flags = [flag for tile in tiles for flag in (tile.lower_x(), tile.upper_x())]
    mask = group_mask(flags, (TS, LANES))
    group = lax.broadcasted_iota(jnp.int32, (TS, LANES), 1) >> 4
    ice[TPD, TOP : TOP + TS, :] = jnp.where(mask, 1.0, 0.0)
    for k, target in enumerate(targets):
        before = pltpu.roll(packs[2, PACK:, :], (LANES - MARGIN * k) % LANES, 1)
        after = pltpu.roll(packs[0, PACK:, :], (LANES - MARGIN - MARGIN * k) % LANES, 1)
        beside = jnp.where(group == 0, before, after)
        for j in range(TPD):
            tile = target[j, TOP : TOP + TS, :]
            if j + 1 < TPD:
                moved = pltpu.roll(tile, (2 * MARGIN * j + 3 * MARGIN) % LANES, 1)
                beside = jnp.where(group == 2 * (j + 1), moved, beside)
            if j:
                moved = pltpu.roll(tile, (2 * MARGIN * j - MARGIN) % LANES, 1)
                beside = jnp.where(group == 2 * (j - 1) + 1, moved, beside)
        target[TPD, TOP : TOP + TS, :] = jnp.where(mask, beside, 1.0 if k == 5 else 0.0)

    chunk = 24
    first_row, last_row = TOP - SECTION, TOP + TS + SECTION
    lane = lax.broadcasted_iota(jnp.int32, (chunk, LANES), 1)
    at_start, at_end = lane == 0, lane == LANES - 1
    in_group = lane & (2 * MARGIN - 1)
    group_pair = lane >> 5
    before_gap, after_gap = in_group == MARGIN - 1, in_group == MARGIN

    def beside_tile(ref, lead, j, rows):
        centre = ref[lead + (j, rows)]
        edge = pltpu.roll(ref[lead + (TPD, rows)], LANES - MARGIN - 2 * MARGIN * j, 1)
        lower = pltpu.roll(jnp.where(at_end, edge, centre), 1, 1)
        upper = pltpu.roll(jnp.where(at_start, edge, centre), LANES - 1, 1)
        return centre, lower, upper

    def beside_columns(ref, lead, j, rows):
        centre = ref[lead + (TPD, rows)]
        edge = pltpu.roll(ref[lead + (0, rows)], MARGIN, 1)
        for t in range(1, TPD):
            moved = pltpu.roll(ref[lead + (t, rows)], (2 * MARGIN * t + MARGIN) % LANES, 1)
            edge = jnp.where(group_pair == t, moved, edge)
        lower = pltpu.roll(jnp.where(before_gap, edge, centre), 1, 1)
        upper = pltpu.roll(jnp.where(after_gap, edge, centre), LANES - 1, 1)
        return centre, lower, upper

    def viscosity(now, j, beside):
        for start in range(first_row, last_row, chunk):
            rows, under, over = (slice(start + k, start + k + chunk) for k in (0, -1, 1))
            _, u_lx, u_ux = beside(u, (now,), j, rows)
            _, v_lx, v_ux = beside(v, (now,), j, rows)
            ux = u_ux - u_lx
            vy = v[now, j, over] - v[now, j, under]
            shear = (u[now, j, over] - u[now, j, under]) + (v_ux - v_lx)
            strain = 0.25 * (ux * ux + vy * vy + ux * vy + 0.25 * shear * shear) + STRAIN_EPSILON
            w[j, rows] = (0.25 * h[j, rows]) * jnp.exp(jnp.log(strain) * (-1.0 / 3.0))

    def quotient(top, bottom):
        guess = pl.reciprocal(bottom, approx=True)
        return top * (guess * (2.0 - bottom * guess))

    def relax(now, j, beside):
        for start in range(first_row, last_row, chunk):
            rows, under, over = (slice(start + k, start + k + chunk) for k in (0, -1, 1))
            here, w_lx, w_ux = beside(w, (), j, rows)
            c_lx, c_ux = here + w_lx, here + w_ux
            c_ly, c_uy = here + w[j, under], here + w[j, over]
            _, u_lx, u_ux = beside(u, (now,), j, rows)
            _, v_lx, v_ux = beside(v, (now,), j, rows)
            c_x, c_y = c_lx + c_ux, c_ly + c_uy
            drag = f[j, rows]
            u_top = 4.0 * (c_lx * u_lx + c_ux * u_ux) + c_ly * u[now, j, under] + c_uy * u[now, j, over] - d0[j, rows]
            v_top = c_lx * v_lx + c_ux * v_ux + 4.0 * (c_ly * v[now, j, under] + c_uy * v[now, j, over]) - d1[j, rows]
            u_new = quotient(u_top, 4.0 * c_x + c_y + drag)
            v_new = quotient(v_top, c_x + 4.0 * c_y + drag)
            if beside is beside_columns or start == first_row or start + chunk == last_row:
                is_ice = ice[j, rows] > 0.0
                u_new = jnp.where(is_ice, u_new, 0.0)
                v_new = jnp.where(is_ice, v_new, 0.0)
            u[1 - now, j, rows] = u_new
            v[1 - now, j, rows] = v_new

    for j in range(TPD):
        ice[j, TOP : TOP + 2 * SECTION, :] = jnp.ones((2 * SECTION, LANES), jnp.float32)
        ice[j, TOP + TS - 2 * SECTION : TOP + TS, :] = jnp.ones((2 * SECTION, LANES), jnp.float32)

    @pl.loop(0, SWEEPS)
    def _(sweep):
        now = sweep & 1

        @pl.loop(0, TPD)
        def _(j):
            viscosity(now, j, beside_tile)

        viscosity(now, TPD, beside_columns)

        @pl.loop(0, TPD)
        def _(j):
            relax(now, j, beside_tile)

        relax(now, TPD, beside_columns)

    last = SWEEPS & 1
    results = [
        pltpu.make_async_copy(u.at[(last,) + own], vel_ref.at[0], sems.at[0]),
        pltpu.make_async_copy(v.at[(last,) + own], vel_ref.at[1], sems.at[1]),
    ]
    for copy in results:
        copy.start()

    @pl.loop(0, TPD)
    def _(j):
        part = 32
        lane = lax.broadcasted_iota(jnp.int32, (part, LANES), 1)
        at_start, at_end = lane == 0, lane == LANES - 1

        def beside_tile(ref, lead, rows):
            centre = ref[lead + (j, rows)]
            edge = pltpu.roll(ref[lead + (TPD, rows)], LANES - MARGIN - 2 * MARGIN * j, 1)
            lower = pltpu.roll(jnp.where(at_end, edge, centre), 1, 1)
            upper = pltpu.roll(jnp.where(at_start, edge, centre), LANES - 1, 1)
            return centre, lower, upper

        for start in range(TOP, TOP + TS, part):
            rows, under, over = (slice(start + k, start + k + part) for k in (0, -1, 1))
            u_c, u_lx, u_ux = beside_tile(u, (last,), rows)
            h_c, h_lx, h_ux = beside_tile(h, (), rows)
            v_c = v[last, j, rows]
            s_lx, s_ux = 0.5 * (u_lx + u_c), 0.5 * (u_c + u_ux)
            s_ly, s_uy = 0.5 * (v[last, j, under] + v_c), 0.5 * (v_c + v[last, j, over])
            flux_lx = jnp.maximum(s_lx, 0.0) * h_lx + jnp.minimum(s_lx, 0.0) * h_c
            flux_ux = jnp.maximum(s_ux, 0.0) * h_c + jnp.minimum(s_ux, 0.0) * h_ux
            flux_ly = jnp.maximum(s_ly, 0.0) * h[j, under] + jnp.minimum(s_ly, 0.0) * h_c
            flux_uy = jnp.maximum(s_uy, 0.0) * h_c + jnp.minimum(s_uy, 0.0) * h[j, over]
            next_ref[j, start - TOP : start - TOP + part, :] = h_c - TIME_STEP * (
                flux_ux - flux_lx + flux_uy - flux_ly
            )

    for copy in results:
        copy.wait()


def shards(slots, thickness, driving, friction, velocity_start, row_lengths):
    f32 = jnp.float32
    vmem = pl.BlockSpec(memory_space=pltpu.VMEM)
    smem = pl.BlockSpec(memory_space=pltpu.SMEM)
    anywhere = pl.BlockSpec(memory_space=pl.ANY)
    params = pltpu.CompilerParams(vmem_limit_bytes=VMEM_LIMIT)
    strips_shape = jax.ShapeDtypeStruct((TPD, STRIP, LANES), f32)
    columns_shape = jax.ShapeDtypeStruct((TS, LANES), f32)
    rows = row_lengths.shape[0]

    with jax.named_scope("strips"):
        bottom, top, right, left = pl.pallas_call(
            strips_kernel,
            out_shape=(strips_shape, strips_shape, columns_shape, columns_shape),
            in_specs=[vmem] * 4,
            out_specs=(vmem,) * 4,
            compiler_params=params,
        )(thickness, driving, friction, velocity_start)

    with jax.named_scope("strides"):
        bottoms = [bottom] + [cyclic_shift(bottom, STRIDE * a) for a in range(1, HOPS)]
        tops = [top] + [cyclic_shift(top, -STRIDE * a) for a in range(1, HOPS)]

    with jax.named_scope("route"):
        back, local, ahead = pl.pallas_call(
            functools.partial(route_kernel, slots),
            out_shape=(
                jax.ShapeDtypeStruct((FULL_PACK, LANES), f32),
                jax.ShapeDtypeStruct((PACK, LANES), f32),
                jax.ShapeDtypeStruct((FULL_PACK, LANES), f32),
            ),
            in_specs=[smem] + [anywhere] * (2 * HOPS) + [vmem] * 2,
            out_specs=(vmem,) * 3,
            scratch_shapes=[
                pltpu.VMEM((2, HOPS, TPD, STRIP, LANES), f32),
                pltpu.SMEM((rows,), jnp.int32),
                pltpu.SemaphoreType.DMA((2 * HOPS,)),
            ],
            compiler_params=params,
        )(row_lengths, *bottoms, *tops, right, left)

    with jax.named_scope("last_step"):
        back = cyclic_shift(back, -1)
        ahead = cyclic_shift(ahead, 1)

    with jax.named_scope("sweeps"):
        field = pltpu.VMEM((TPD + 1, ROWS, LANES), f32)
        pair = pltpu.VMEM((2, TPD + 1, ROWS, LANES), f32)
        velocity, thickness_next = pl.pallas_call(
            functools.partial(sweeps_kernel, slots),
            out_shape=(
                jax.ShapeDtypeStruct(velocity_start.shape, f32),
                jax.ShapeDtypeStruct(thickness.shape, f32),
            ),
            in_specs=[smem] + [anywhere] * 7,
            out_specs=(anywhere, vmem),
            scratch_shapes=[
                pair, pair, field, field, field, field, field, field,
                pltpu.VMEM((3, FULL_PACK, LANES), f32),
                pltpu.SMEM((rows,), jnp.int32),
                pltpu.SemaphoreType.DMA((9,)),
            ],
            compiler_params=params,
        )(row_lengths, thickness, driving, friction, velocity_start, back, local, ahead)
    return velocity, thickness_next


def solution(mesh):
    in_specs = (
        P("ta", None, None),
        P(None, "ta", None, None),
        P(("ma", "ta"), None, None),
        P(None, "ta", None, None),
        P(),
    )
    out_specs = (P(None, ("ma", "ta"), None, None), P(("ma", "ta"), None, None))
    slots = TPD * mesh.shape["ta"]
    return jax.shard_map(
        functools.partial(shards, slots), mesh=mesh, in_specs=in_specs, out_specs=out_specs, check_vma=False
    )
```

```python
import functools

import jax
import jax.numpy as jnp
from jax import lax
from jax.experimental import pallas as pl
from jax.experimental.pallas import tpu as pltpu
from jax.sharding import PartitionSpec as P


GC = 48
SWEEPS = 4
STRAIN_EPSILON = 0.01
TIME_STEP = 0.1

TS = 128
LANES = 128
TPD = 4
SECTION = 8
STRIP = 6 * SECTION
TOP = 16
ROWS = TS + 2 * TOP
MARGIN = 16
STRIDE = 3
HOPS = 5
MAIN_BLOCKS = 2 * TPD
PACK = (MAIN_BLOCKS + 2) * STRIP
FULL_PACK = PACK + TS
VMEM_LIMIT = 40 * 1024 * 1024


def cyclic_shift(value, steps):
    count = lax.axis_size("ta")
    return lax.ppermute(value, "ta", [(i, (i + steps) % count) for i in range(count)])


def fill_row_ends(len_ref, ends_ref):
    total = jnp.int32(0)
    ends = []
    for r in range(len_ref.shape[0]):
        total = total + len_ref[r]
        ends_ref[r] = total
        ends.append(total)
    return ends


class Tile:
    def __init__(self, len_ref, ends_ref, ends, slot, slots):
        rows = len_ref.shape[0]
        row = jnp.int32(0)
        for end in ends:
            row = row + jnp.where(end <= slot, 1, 0)
        self.slot = slot
        self.real = (slot >= 0) & (slot < slots)
        row = jnp.minimum(row, rows - 1)
        self.length = len_ref[row]
        self.above = jnp.where(row >= 1, len_ref[jnp.maximum(row - 1, 0)], 0)
        self.below = jnp.where(row < rows - 1, len_ref[jnp.minimum(row + 1, rows - 1)], 0)
        self.column = GC + slot - ends_ref[row]

    def side(self, down, step):
        column = self.column + step
        length = self.below if down else self.above
        there = self.real & (column < GC) & (column >= GC - length)
        slot = self.slot + (self.below if down else -self.length) + step
        return there, slot

    def lower_x(self):
        return self.real & (self.column > GC - self.length)

    def upper_x(self):
        return self.real & (self.column < GC - 1)


def hop(device, slot, down):
    owner = slot >> 2
    q = jnp.maximum((owner - device) if down else (device - owner), 0)
    a = jnp.minimum(((q + 1) * 11) >> 5, HOPS - 1)
    b = q - STRIDE * a
    return a, (-b if down else b)


def strips_kernel(h_ref, d_ref, f_ref, v_ref, bottom_ref, top_ref, right_ref, left_ref):
    fields = [v_ref.at[0], v_ref.at[1], h_ref, d_ref.at[0], d_ref.at[1], f_ref]
    row = lax.broadcasted_iota(jnp.int32, (SECTION, LANES), 0)
    lane = lax.broadcasted_iota(jnp.int32, (TS, LANES), 1)
    for t in range(TPD):
        for k, field in enumerate(fields):
            last = field[t, TS - SECTION :, :]
            first = field[t, :SECTION, :]
            if k in (3, 4):
                extra = fields[k - 3]
                last = jnp.where(row == 0, extra[t, TS - SECTION - 1 : TS - SECTION, :], last)
                first = jnp.where(row == SECTION - 1, extra[t, SECTION : SECTION + 1, :], first)
            bottom_ref[t, k * SECTION : (k + 1) * SECTION, :] = last
            top_ref[t, k * SECTION : (k + 1) * SECTION, :] = first
    right = jnp.zeros((TS, LANES), jnp.float32)
    left = jnp.zeros((TS, LANES), jnp.float32)
    for k, field in enumerate(fields):
        here = (lane >> 4) == k
        right = jnp.where(here, pltpu.roll(field[TPD - 1], (MARGIN * k + MARGIN) % LANES, 1), right)
        left = jnp.where(here, pltpu.roll(field[0], MARGIN * k, 1) if k else field[0], left)
    right_ref[...] = right
    left_ref[...] = left


def route_kernel(slots, len_ref, *refs):
    given = refs[: 2 * HOPS]
    right_ref, left_ref = refs[2 * HOPS : 2 * HOPS + 2]
    outs = refs[2 * HOPS + 2 : 2 * HOPS + 5]
    strips, ends_ref, sems = refs[2 * HOPS + 5 :]
    copies = [
        pltpu.make_async_copy(given[i], strips.at[i // HOPS, i % HOPS], sems.at[i]) for i in range(2 * HOPS)
    ]
    for copy in copies:
        copy.start()
    ends = fill_row_ends(len_ref, ends_ref)
    outs[0][PACK:, :] = left_ref[...]
    outs[2][PACK:, :] = right_ref[...]
    for out in outs:
        out[MAIN_BLOCKS * STRIP : PACK, :] = jnp.zeros((2 * STRIP, LANES), jnp.float32)
    lane = lax.broadcasted_iota(jnp.int32, (STRIP, LANES), 1)
    me, count = lax.axis_index("ta"), slots // TPD
    for copy in copies:
        copy.wait()
    for step, out in zip((-1, 0, 1), outs):
        device = lax.rem(me + step + count, count)
        for j in range(TPD):
            tile = Tile(len_ref, ends_ref, ends, device * TPD + j, slots)
            for down in (0, 1):
                for across in (-1, 0, 1):
                    there, slot = tile.side(down, across)
                    a, shift = hop(device, slot, down)

                    @pl.when(there & (shift == step))
                    def _(out=out, j=j, down=down, across=across, a=a, slot=slot):
                        moved = pltpu.roll(strips[down, a, slot & 3], 2 * MARGIN * j + MARGIN, 1)
                        if across == 0:
                            block = down * TPD + j
                            out[block * STRIP : (block + 1) * STRIP, :] = moved
                        else:
                            block = MAIN_BLOCKS + down
                            first = 2 * j + (across + 1) // 2
                            rows = slice(block * STRIP, (block + 1) * STRIP)
                            out[rows, :] = jnp.where((lane >> 4) == first, moved, out[rows, :])


def group_mask(flags, shape):
    bits = jnp.int32(0)
    for k, flag in enumerate(flags):
        bits = bits + jnp.where(flag, 1 << k, 0)
    group = lax.broadcasted_iota(jnp.int32, shape, 1) >> 4
    return ((jnp.full(shape, bits) >> group) & 1) == 1


def sweeps_kernel(
    slots, len_ref, h_ref, d_ref, f_ref, v_ref, back_ref, local_ref, ahead_ref,
    vel_ref, next_ref, u, v, u_other, v_other, w, h, d0, d1, f, ice,
    u_low, u_high, v_low, v_high, results, packs, ends_ref, sems, out_sems,
):
    own = (pl.ds(0, TPD), pl.ds(TOP, TS))
    copies = [
        (v_ref.at[0], u.at[own]),
        (v_ref.at[1], v.at[own]),
        (h_ref, h.at[own]),
        (d_ref.at[0], d0.at[own]),
        (d_ref.at[1], d1.at[own]),
        (f_ref, f.at[own]),
        (back_ref, packs.at[0]),
        (local_ref, packs.at[1, pl.ds(0, PACK)]),
        (ahead_ref, packs.at[2]),
    ]
    copies = [pltpu.make_async_copy(a, b, sems.at[i]) for i, (a, b) in enumerate(copies)]
    for copy in copies:
        copy.start()
    me = lax.axis_index("ta")
    ends = fill_row_ends(len_ref, ends_ref)
    tiles = [Tile(len_ref, ends_ref, ends, me * TPD + j, slots) for j in range(TPD)]
    zero = jnp.zeros((SECTION, LANES), jnp.float32)
    one = jnp.ones((SECTION, LANES), jnp.float32)
    for block in range(TPD + 1):
        for start in (0, ROWS - SECTION):
            rows = slice(start, start + SECTION)
            u[block, rows, :] = zero
            v[block, rows, :] = zero
            w[block, rows, :] = zero
    for copy in copies:
        copy.wait()

    targets = (u, v, h, d0, d1, f)
    for down in (0, 1):
        start = TOP + TS if down else TOP - SECTION
        rows = slice(start, start + SECTION)
        deep = SECTION - 1 if down else 0
        far = start + SECTION if down else start - 1
        for j in range(TPD + 1):
            if j < TPD:
                there, slot = tiles[j].side(down, 0)
                _, shift = hop(me, slot, down)
                which = jnp.where(there, shift + 1, 1)
                base = (down * TPD + j) * STRIP
                parts = [packs[which, base + k * SECTION : base + (k + 1) * SECTION, :] for k in range(6)]
                mask = jnp.full((SECTION, LANES), jnp.where(there, 1, 0)) == 1
            else:
                base = (MAIN_BLOCKS + down) * STRIP
                parts = [
                    packs[0, base + k * SECTION : base + (k + 1) * SECTION, :]
                    + packs[1, base + k * SECTION : base + (k + 1) * SECTION, :]
                    + packs[2, base + k * SECTION : base + (k + 1) * SECTION, :]
                    for k in range(6)
                ]
                flags = [tile.side(down, across)[0] for tile in tiles for across in (-1, 1)]
                mask = group_mask(flags, (SECTION, LANES))
            for k, target in enumerate(targets):
                target[j, rows, :] = jnp.where(mask, parts[k], one if k == 5 else zero)
            for k in (0, 1):
                line = jnp.where(mask, parts[3 + k], zero)
                targets[k][j, far : far + 1, :] = line[deep : deep + 1, :]
            ice[j, rows, :] = jnp.where(mask, one, zero)

    flags = [flag for tile in tiles for flag in (tile.lower_x(), tile.upper_x())]
    mask = group_mask(flags, (TS, LANES))
    lane = lax.broadcasted_iota(jnp.int32, (TS, LANES), 1)
    group, group_pair = lane >> 4, lane >> 5
    middle = slice(TOP, TOP + TS)
    ice[TPD, middle, :] = jnp.where(mask, 1.0, 0.0)
    for k, target in enumerate(targets):
        edges = None
        for j in range(TPD):
            tile = pltpu.roll(target[j, middle, :], 2 * MARGIN * j + MARGIN, 1)
            target[j, middle, :] = tile
            edges = tile if j == 0 else jnp.where(group_pair == j, tile, edges)
        before = pltpu.roll(packs[2, PACK:, :], (LANES - MARGIN * k) % LANES, 1)
        after = pltpu.roll(packs[0, PACK:, :], (LANES - MARGIN - MARGIN * k) % LANES, 1)
        lower = jnp.where(group == 0, before, pltpu.roll(edges, 2 * MARGIN, 1))
        upper = jnp.where(group == 2 * TPD - 1, after, pltpu.roll(edges, LANES - 2 * MARGIN, 1))
        beside = jnp.where((group & 1) == 0, lower, upper)
        target[TPD, middle, :] = jnp.where(mask, beside, 1.0 if k == 5 else 0.0)

    chunk = 72
    first_row, last_row = TOP - SECTION, TOP + TS + SECTION

    def in_tile(ref, j, rows):
        centre, edge = ref[j, rows], ref[TPD, rows]
        lane = lax.broadcasted_iota(jnp.int32, centre.shape, 1)
        high_side = 2 * MARGIN * j + MARGIN
        lower = pltpu.roll(jnp.where(lane == high_side - 1, edge, centre), 1, 1)
        upper = pltpu.roll(jnp.where(lane == high_side, edge, centre), LANES - 1, 1)
        return centre, lower, upper

    def in_columns(ref, j, rows):
        centre, edge = ref[TPD, rows], ref[0, rows]
        lane = lax.broadcasted_iota(jnp.int32, centre.shape, 1)
        for t in range(1, TPD):
            edge = jnp.where((lane >> 5) == t, ref[t, rows], edge)
        within = lane & (2 * MARGIN - 1)
        lower = pltpu.roll(jnp.where(within == MARGIN - 1, edge, centre), 1, 1)
        upper = pltpu.roll(jnp.where(within == MARGIN, edge, centre), LANES - 1, 1)
        return centre, lower, upper

    def viscosity(u, v, j, beside):
        for start in range(first_row, last_row, chunk):
            rows, under, over = (slice(start + k, start + k + chunk) for k in (0, -1, 1))
            _, u_lx, u_ux = beside(u, j, rows)
            _, v_lx, v_ux = beside(v, j, rows)
            u_low[j, rows], u_high[j, rows] = u_lx, u_ux
            v_low[j, rows], v_high[j, rows] = v_lx, v_ux
            ux = u_ux - u_lx
            vy = v[j, over] - v[j, under]
            shear = (u[j, over] - u[j, under]) + (v_ux - v_lx)
            strain = 0.25 * (ux * ux + vy * vy + ux * vy + 0.25 * shear * shear) + STRAIN_EPSILON
            w[j, rows] = (0.25 * h[j, rows]) * jnp.exp(jnp.log(strain) * (-1.0 / 3.0))

    def quotient(top, bottom):
        guess = pl.reciprocal(bottom, approx=True)
        return top * (guess * (2.0 - bottom * guess))

    def relax(u, v, u_next, v_next, j, beside):
        for start in range(first_row, last_row, chunk):
            rows, under, over = (slice(start + k, start + k + chunk) for k in (0, -1, 1))
            here, w_lx, w_ux = beside(w, j, rows)
            c_lx, c_ux = here + w_lx, here + w_ux
            c_ly, c_uy = here + w[j, under], here + w[j, over]
            u_lx, u_ux = u_low[j, rows], u_high[j, rows]
            v_lx, v_ux = v_low[j, rows], v_high[j, rows]
            c_x, c_y = c_lx + c_ux, c_ly + c_uy
            drag = f[j, rows]
            u_top = 4.0 * (c_lx * u_lx + c_ux * u_ux) + c_ly * u[j, under] + c_uy * u[j, over] - d0[j, rows]
            v_top = c_lx * v_lx + c_ux * v_ux + 4.0 * (c_ly * v[j, under] + c_uy * v[j, over]) - d1[j, rows]
            u_new = quotient(u_top, 4.0 * c_x + c_y + drag)
            v_new = quotient(v_top, c_x + 4.0 * c_y + drag)
            if beside is in_columns or start == first_row or start + chunk == last_row:
                is_ice = ice[j, rows] > 0.0
                u_new = jnp.where(is_ice, u_new, 0.0)
                v_new = jnp.where(is_ice, v_new, 0.0)
            u_next[j, rows] = u_new
            v_next[j, rows] = v_new

    for j in range(TPD):
        ice[j, middle, :] = jnp.ones((TS, LANES), jnp.float32)

    def sweep(*state):
        @pl.loop(0, TPD)
        def _(j):
            viscosity(*state[:2], j, in_tile)

        viscosity(*state[:2], TPD, in_columns)

        @pl.loop(0, TPD)
        def _(j):
            relax(*state, j, in_tile)

        relax(*state, TPD, in_columns)

    @pl.loop(0, SWEEPS // 2)
    def _(_):
        sweep(u, v, u_other, v_other)
        sweep(u_other, v_other, u, v)

    def given(j):
        refs = (vel_ref.at[0, j], vel_ref.at[1, j], next_ref.at[j])
        return [pltpu.make_async_copy(results.at[k, j], ref, out_sems.at[k, j]) for k, ref in enumerate(refs)]

    @pl.loop(0, TPD)
    def _(j):
        part = 64
        back = LANES - MARGIN - 2 * MARGIN * j

        for start in range(TOP, TOP + TS, part):
            rows, under, over = (slice(start + k, start + k + part) for k in (0, -1, 1))
            u_c, u_lx, u_ux = in_tile(u, j, rows)
            h_c, h_lx, h_ux = in_tile(h, j, rows)
            v_c = v[j, rows]
            s_lx, s_ux = 0.5 * (u_lx + u_c), 0.5 * (u_c + u_ux)
            s_ly, s_uy = 0.5 * (v[j, under] + v_c), 0.5 * (v_c + v[j, over])
            flux_lx = jnp.maximum(s_lx, 0.0) * h_lx + jnp.minimum(s_lx, 0.0) * h_c
            flux_ux = jnp.maximum(s_ux, 0.0) * h_c + jnp.minimum(s_ux, 0.0) * h_ux
            flux_ly = jnp.maximum(s_ly, 0.0) * h[j, under] + jnp.minimum(s_ly, 0.0) * h_c
            flux_uy = jnp.maximum(s_uy, 0.0) * h_c + jnp.minimum(s_uy, 0.0) * h[j, over]
            h_next = h_c - TIME_STEP * (flux_ux - flux_lx + flux_uy - flux_ly)
            for k, value in enumerate((u_c, v_c, h_next)):
                results[k, j, start - TOP : start - TOP + part, :] = pltpu.roll(value, back, 1)
        for copy in given(j):
            copy.start()

    for j in range(TPD):
        for copy in given(j):
            copy.wait()


def shards(slots, thickness, driving, friction, velocity_start, row_lengths):
    f32 = jnp.float32
    vmem = pl.BlockSpec(memory_space=pltpu.VMEM)
    smem = pl.BlockSpec(memory_space=pltpu.SMEM)
    anywhere = pl.BlockSpec(memory_space=pl.ANY)
    params = pltpu.CompilerParams(vmem_limit_bytes=VMEM_LIMIT)
    strips_shape = jax.ShapeDtypeStruct((TPD, STRIP, LANES), f32)
    columns_shape = jax.ShapeDtypeStruct((TS, LANES), f32)
    rows = row_lengths.shape[0]

    with jax.named_scope("strips"):
        bottom, top, right, left = pl.pallas_call(
            strips_kernel,
            out_shape=(strips_shape, strips_shape, columns_shape, columns_shape),
            in_specs=[vmem] * 4,
            out_specs=(vmem,) * 4,
            compiler_params=params,
        )(thickness, driving, friction, velocity_start)

    with jax.named_scope("strides"):
        bottoms = [bottom] + [cyclic_shift(bottom, STRIDE * a) for a in range(1, HOPS)]
        tops = [top] + [cyclic_shift(top, -STRIDE * a) for a in range(1, HOPS)]

    with jax.named_scope("route"):
        back, local, ahead = pl.pallas_call(
            functools.partial(route_kernel, slots),
            out_shape=(
                jax.ShapeDtypeStruct((FULL_PACK, LANES), f32),
                jax.ShapeDtypeStruct((PACK, LANES), f32),
                jax.ShapeDtypeStruct((FULL_PACK, LANES), f32),
            ),
            in_specs=[smem] + [anywhere] * (2 * HOPS) + [vmem] * 2,
            out_specs=(vmem,) * 3,
            scratch_shapes=[
                pltpu.VMEM((2, HOPS, TPD, STRIP, LANES), f32),
                pltpu.SMEM((rows,), jnp.int32),
                pltpu.SemaphoreType.DMA((2 * HOPS,)),
            ],
            compiler_params=params,
        )(row_lengths, *bottoms, *tops, right, left)

    with jax.named_scope("last_step"):
        back = cyclic_shift(back, -1)
        ahead = cyclic_shift(ahead, 1)

    with jax.named_scope("sweeps"):
        field = pltpu.VMEM((TPD + 1, ROWS, LANES), f32)
        velocity, thickness_next = pl.pallas_call(
            functools.partial(sweeps_kernel, slots),
            out_shape=(
                jax.ShapeDtypeStruct(velocity_start.shape, f32),
                jax.ShapeDtypeStruct(thickness.shape, f32),
            ),
            in_specs=[smem] + [anywhere] * 7,
            out_specs=(anywhere, anywhere),
            scratch_shapes=[
                *[field] * 14,
                pltpu.VMEM((3, TPD, TS, LANES), f32),
                pltpu.VMEM((3, FULL_PACK, LANES), f32),
                pltpu.SMEM((rows,), jnp.int32),
                pltpu.SemaphoreType.DMA((9,)),
                pltpu.SemaphoreType.DMA((3, TPD)),
            ],
            compiler_params=params,
        )(row_lengths, thickness, driving, friction, velocity_start, back, local, ahead)
    return velocity, thickness_next


def solution(mesh):
    in_specs = (
        P("ta", None, None),
        P(None, "ta", None, None),
        P(("ma", "ta"), None, None),
        P(None, "ta", None, None),
        P(),
    )
    out_specs = (P(None, ("ma", "ta"), None, None), P(("ma", "ta"), None, None))
    slots = TPD * mesh.shape["ta"]
    return jax.shard_map(
        functools.partial(shards, slots), mesh=mesh, in_specs=in_specs, out_specs=out_specs, check_vma=False
    )
```

```python
import functools

import jax
import jax.numpy as jnp
from jax import lax
from jax.experimental import pallas as pl
from jax.experimental.pallas import tpu as pltpu
from jax.sharding import PartitionSpec as P


GC = 48
SWEEPS = 4
STRAIN_EPSILON = 0.01
TIME_STEP = 0.1

TS = 128
LANES = 128
TPD = 4
SECTION = 8
STRIP = 6 * SECTION
TOP = 16
ROWS = TS + 2 * TOP
MARGIN = 16
STRIDE = 3
HOPS = 5
MAIN_BLOCKS = 2 * TPD
PACK = (MAIN_BLOCKS + 2) * STRIP
FULL_PACK = PACK + TS
VMEM_LIMIT = 40 * 1024 * 1024
FIRST_VMEM_LIMIT = 60 * 1024 * 1024
ROUTE = 3 * TPD * 2 * 3
WHICH = ROUTE
BITS = WHICH + 2 * TPD
PLAN = 128


def cyclic_shift(value, steps):
    count = lax.axis_size("ta")
    return lax.ppermute(value, "ta", [(i, (i + steps) % count) for i in range(count)])


def fill_row_ends(len_ref, ends_ref):
    total = jnp.int32(0)
    ends = []
    for r in range(len_ref.shape[0]):
        total = total + len_ref[r]
        ends_ref[r] = total
        ends.append(total)
    return ends


class Tile:
    def __init__(self, len_ref, ends_ref, ends, slot, slots):
        rows = len_ref.shape[0]
        row = jnp.int32(0)
        for end in ends:
            row = row + jnp.where(end <= slot, 1, 0)
        self.slot = slot
        self.real = (slot >= 0) & (slot < slots)
        row = jnp.minimum(row, rows - 1)
        self.length = len_ref[row]
        self.above = jnp.where(row >= 1, len_ref[jnp.maximum(row - 1, 0)], 0)
        self.below = jnp.where(row < rows - 1, len_ref[jnp.minimum(row + 1, rows - 1)], 0)
        self.column = GC + slot - ends_ref[row]

    def side(self, down, step):
        column = self.column + step
        length = self.below if down else self.above
        there = self.real & (column < GC) & (column >= GC - length)
        slot = self.slot + (self.below if down else -self.length) + step
        return there, slot

    def lower_x(self):
        return self.real & (self.column > GC - self.length)

    def upper_x(self):
        return self.real & (self.column < GC - 1)


def hop(device, slot, down):
    owner = slot >> 2
    q = jnp.maximum((owner - device) if down else (device - owner), 0)
    a = jnp.minimum(((q + 1) * 11) >> 5, HOPS - 1)
    b = q - STRIDE * a
    return a, (-b if down else b)


def field_refs(h_ref, d_ref, f_ref, v_ref):
    return [v_ref.at[0], v_ref.at[1], h_ref, d_ref.at[0], d_ref.at[1], f_ref]


def put_strips(ends, bottom_ref, top_ref):
    row = lax.broadcasted_iota(jnp.int32, (SECTION, LANES), 0)
    for t in range(TPD):
        for k in range(6):
            last = ends(k, t, slice(TS - SECTION, TS))
            first = ends(k, t, slice(0, SECTION))
            if k in (3, 4):
                last = jnp.where(row == 0, ends(k - 3, t, slice(TS - SECTION - 1, TS - SECTION)), last)
                first = jnp.where(row == SECTION - 1, ends(k - 3, t, slice(SECTION, SECTION + 1)), first)
            bottom_ref[t, k * SECTION : (k + 1) * SECTION, :] = last
            top_ref[t, k * SECTION : (k + 1) * SECTION, :] = first


def sent_strips_kernel(h_ref, d_ref, f_ref, v_ref, bottom_ref, top_ref, held, sems):
    copies = []
    for k, ref in enumerate(field_refs(h_ref, d_ref, f_ref, v_ref)):
        copies += [
            pltpu.make_async_copy(ref.at[:, pl.ds(0, 2 * SECTION)], held.at[0, k], sems.at[0, k]),
            pltpu.make_async_copy(ref.at[:, pl.ds(TS - 2 * SECTION, 2 * SECTION)], held.at[1, k], sems.at[1, k]),
        ]
    for copy in copies:
        copy.start()
    for copy in copies:
        copy.wait()

    def ends(k, t, rows):
        if rows.start < 2 * SECTION:
            return held[0, k, t, rows, :]
        return held[1, k, t, rows.start - TS + 2 * SECTION : rows.stop - TS + 2 * SECTION, :]

    put_strips(ends, bottom_ref, top_ref)


def own_strips_kernel(h_ref, d_ref, f_ref, v_ref, bottom_ref, top_ref, right_ref, left_ref):
    fields = field_refs(h_ref, d_ref, f_ref, v_ref)
    put_strips(lambda k, t, rows: fields[k][t, rows, :], bottom_ref, top_ref)
    lane = lax.broadcasted_iota(jnp.int32, (TS, LANES), 1)
    right = jnp.zeros((TS, LANES), jnp.float32)
    left = jnp.zeros((TS, LANES), jnp.float32)
    for k, field in enumerate(fields):
        here = (lane >> 4) == k
        right = jnp.where(here, pltpu.roll(field[TPD - 1], (MARGIN * k + MARGIN) % LANES, 1), right)
        left = jnp.where(here, pltpu.roll(field[0], MARGIN * k, 1) if k else field[0], left)
    right_ref[...] = right
    left_ref[...] = left


def plan_kernel(slots, len_ref, out_ref, plan_ref, ends_ref, sem):
    ends = fill_row_ends(len_ref, ends_ref)
    me, count = lax.axis_index("ta"), slots // TPD
    for step in (-1, 0, 1):
        device = lax.rem(me + step + count, count)
        tiles = [Tile(len_ref, ends_ref, ends, device * TPD + j, slots) for j in range(TPD)]
        for j, tile in enumerate(tiles):
            for down in (0, 1):
                for across in (-1, 0, 1):
                    there, slot = tile.side(down, across)
                    a, shift = hop(device, slot, down)
                    entry = (((step + 1) * TPD + j) * 2 + down) * 3 + across + 1
                    plan_ref[entry] = jnp.where(there & (shift == step), TPD * a + (slot & 3), -1)
                    if step == 0 and across == 0:
                        plan_ref[WHICH + down * TPD + j] = jnp.where(there, shift + 1, -1)
        if step == 0:
            for down in (0, 1):
                plan_ref[BITS + down] = flag_bits([t.side(down, k)[0] for t in tiles for k in (-1, 1)])
            plan_ref[BITS + 2] = flag_bits([flag for t in tiles for flag in (t.lower_x(), t.upper_x())])
    for unused in range(BITS + 3, PLAN):
        plan_ref[unused] = 0
    copy = pltpu.make_async_copy(plan_ref, out_ref, sem)
    copy.start()
    copy.wait()


def flag_bits(flags):
    bits = jnp.int32(0)
    for k, flag in enumerate(flags):
        bits = bits + jnp.where(flag, 1 << k, 0)
    return bits


def own_fields_kernel(h_ref, d_ref, f_ref, v_ref, *outs):
    group = lax.broadcasted_iota(jnp.int32, (TS, LANES), 1) >> 4
    middle = slice(TOP, TOP + TS)
    for ref, out in zip(field_refs(h_ref, d_ref, f_ref, v_ref), outs):
        edges = None
        for j in range(TPD):
            tile = pltpu.roll(ref[j], 2 * MARGIN * j + MARGIN, 1)
            out[j, middle, :] = tile
            edges = tile if j == 0 else jnp.where((group >> 1) == j, tile, edges)
        lower, upper = pltpu.roll(edges, 2 * MARGIN, 1), pltpu.roll(edges, LANES - 2 * MARGIN, 1)
        out[TPD, middle, :] = jnp.where((group & 1) == 0, lower, upper)


def route_kernel(plan_hbm, *refs):
    given = refs[: 2 * HOPS]
    right_ref, left_ref = refs[2 * HOPS : 2 * HOPS + 2]
    outs = refs[2 * HOPS + 2 : 2 * HOPS + 5]
    plan_ref, sem = refs[2 * HOPS + 5 :]
    copy = pltpu.make_async_copy(plan_hbm, plan_ref, sem)
    copy.start()
    outs[0][PACK:, :] = left_ref[...]
    outs[2][PACK:, :] = right_ref[...]
    for out in outs:
        out[MAIN_BLOCKS * STRIP : PACK, :] = jnp.zeros((2 * STRIP, LANES), jnp.float32)
    lane = lax.broadcasted_iota(jnp.int32, (STRIP, LANES), 1)
    copy.wait()
    for step, out in enumerate(outs):
        for down in (0, 1):
            for across in (-1, 0, 1):

                @pl.loop(0, TPD)
                def _(j, step=step, out=out, down=down, across=across):
                    source = plan_ref[((step * TPD + j) * 2 + down) * 3 + across + 1]

                    @pl.when(source >= 0)
                    def _():
                        for a in range(HOPS):

                            @pl.when((source >> 2) == a)
                            def _():
                                strip = given[down * HOPS + a][source & 3]
                                moved = pltpu.roll(strip, 2 * MARGIN * j + MARGIN, 1)
                                if across == 0:
                                    out[pl.ds(pl.multiple_of((down * TPD + j) * STRIP, 8), STRIP), :] = moved
                                else:
                                    rows = slice((MAIN_BLOCKS + down) * STRIP, (MAIN_BLOCKS + down + 1) * STRIP)
                                    here = (lane >> 4) == 2 * j + (across + 1) // 2
                                    out[rows, :] = jnp.where(here, moved, out[rows, :])


def group_mask(bits, shape):
    group = lax.broadcasted_iota(jnp.int32, shape, 1) >> 4
    return ((jnp.full(shape, bits) >> group) & 1) == 1


def sweeps_kernel(plan_ref, ahead_ref, local_ref, back_ref, *refs):
    vel_ref, next_ref, u, v, h, d0, d1, f = refs[6:14]
    u_other, v_other, w, ice, u_low, u_high, v_low, v_high, results, packs, sems, out_sems = refs[14:]
    copies = [
        (back_ref, packs.at[0]),
        (local_ref, packs.at[1, pl.ds(0, PACK)]),
        (ahead_ref, packs.at[2]),
    ]
    copies = [pltpu.make_async_copy(a, b, sems.at[i]) for i, (a, b) in enumerate(copies)]
    for copy in copies:
        copy.start()
    zero = jnp.zeros((SECTION, LANES), jnp.float32)
    one = jnp.ones((SECTION, LANES), jnp.float32)
    for block in range(TPD + 1):
        for start in (0, ROWS - SECTION):
            rows = slice(start, start + SECTION)
            u[block, rows, :] = zero
            v[block, rows, :] = zero
            w[block, rows, :] = zero
    for copy in copies:
        copy.wait()

    targets = (u, v, h, d0, d1, f)
    for down in (0, 1):
        start = TOP + TS if down else TOP - SECTION
        rows = slice(start, start + SECTION)
        deep = SECTION - 1 if down else 0
        far = start + SECTION if down else start - 1
        for j in range(TPD + 1):
            if j < TPD:
                which = plan_ref[WHICH + down * TPD + j]
                there = which >= 0
                which = jnp.maximum(which, 0)
                base = (down * TPD + j) * STRIP
                parts = [packs[which, base + k * SECTION : base + (k + 1) * SECTION, :] for k in range(6)]
                mask = jnp.full((SECTION, LANES), jnp.where(there, 1, 0)) == 1
            else:
                base = (MAIN_BLOCKS + down) * STRIP
                parts = [
                    packs[0, base + k * SECTION : base + (k + 1) * SECTION, :]
                    + packs[1, base + k * SECTION : base + (k + 1) * SECTION, :]
                    + packs[2, base + k * SECTION : base + (k + 1) * SECTION, :]
                    for k in range(6)
                ]
                mask = group_mask(plan_ref[BITS + down], (SECTION, LANES))
            for k, target in enumerate(targets):
                target[j, rows, :] = jnp.where(mask, parts[k], one if k == 5 else zero)
            for k in (0, 1):
                line = jnp.where(mask, parts[3 + k], zero)
                targets[k][j, far : far + 1, :] = line[deep : deep + 1, :]
            ice[j, rows, :] = jnp.where(mask, one, zero)

    mask = group_mask(plan_ref[BITS + 2], (TS, LANES))
    group = lax.broadcasted_iota(jnp.int32, (TS, LANES), 1) >> 4
    middle = slice(TOP, TOP + TS)
    ice[TPD, middle, :] = jnp.where(mask, 1.0, 0.0)
    for k, target in enumerate(targets):
        before = pltpu.roll(packs[2, PACK:, :], (LANES - MARGIN * k) % LANES, 1)
        after = pltpu.roll(packs[0, PACK:, :], (LANES - MARGIN - MARGIN * k) % LANES, 1)
        beside = jnp.where(group == 0, before, target[TPD, middle, :])
        beside = jnp.where(group == 2 * TPD - 1, after, beside)
        target[TPD, middle, :] = jnp.where(mask, beside, 1.0 if k == 5 else 0.0)

    chunk = 72
    first_row, last_row = TOP - SECTION, TOP + TS + SECTION

    def in_tile(ref, j, rows):
        centre, edge = ref[j, rows], ref[TPD, rows]
        lane = lax.broadcasted_iota(jnp.int32, centre.shape, 1)
        high_side = 2 * MARGIN * j + MARGIN
        lower = pltpu.roll(jnp.where(lane == high_side - 1, edge, centre), 1, 1)
        upper = pltpu.roll(jnp.where(lane == high_side, edge, centre), LANES - 1, 1)
        return centre, lower, upper

    def in_columns(ref, j, rows):
        centre, edge = ref[TPD, rows], ref[0, rows]
        lane = lax.broadcasted_iota(jnp.int32, centre.shape, 1)
        for t in range(1, TPD):
            edge = jnp.where((lane >> 5) == t, ref[t, rows], edge)
        within = lane & (2 * MARGIN - 1)
        lower = pltpu.roll(jnp.where(within == MARGIN - 1, edge, centre), 1, 1)
        upper = pltpu.roll(jnp.where(within == MARGIN, edge, centre), LANES - 1, 1)
        return centre, lower, upper

    def viscosity(u, v, j, beside):
        for start in range(first_row, last_row, chunk):
            rows, under, over = (slice(start + k, start + k + chunk) for k in (0, -1, 1))
            _, u_lx, u_ux = beside(u, j, rows)
            _, v_lx, v_ux = beside(v, j, rows)
            u_low[j, rows], u_high[j, rows] = u_lx, u_ux
            v_low[j, rows], v_high[j, rows] = v_lx, v_ux
            ux = u_ux - u_lx
            vy = v[j, over] - v[j, under]
            shear = (u[j, over] - u[j, under]) + (v_ux - v_lx)
            strain = 0.25 * (ux * ux + vy * vy + ux * vy + 0.25 * shear * shear) + STRAIN_EPSILON
            w[j, rows] = (0.25 * h[j, rows]) * jnp.exp(jnp.log(strain) * (-1.0 / 3.0))

    def quotient(top, bottom):
        guess = pl.reciprocal(bottom, approx=True)
        return top * (guess * (2.0 - bottom * guess))

    def relax(u, v, u_next, v_next, j, beside):
        for start in range(first_row, last_row, chunk):
            rows, under, over = (slice(start + k, start + k + chunk) for k in (0, -1, 1))
            here, w_lx, w_ux = beside(w, j, rows)
            c_lx, c_ux = here + w_lx, here + w_ux
            c_ly, c_uy = here + w[j, under], here + w[j, over]
            u_lx, u_ux = u_low[j, rows], u_high[j, rows]
            v_lx, v_ux = v_low[j, rows], v_high[j, rows]
            c_x, c_y = c_lx + c_ux, c_ly + c_uy
            drag = f[j, rows]
            u_top = 4.0 * (c_lx * u_lx + c_ux * u_ux) + c_ly * u[j, under] + c_uy * u[j, over] - d0[j, rows]
            v_top = c_lx * v_lx + c_ux * v_ux + 4.0 * (c_ly * v[j, under] + c_uy * v[j, over]) - d1[j, rows]
            u_new = quotient(u_top, 4.0 * c_x + c_y + drag)
            v_new = quotient(v_top, c_x + 4.0 * c_y + drag)
            if beside is in_columns or start == first_row or start + chunk == last_row:
                is_ice = ice[j, rows] > 0.0
                u_new = jnp.where(is_ice, u_new, 0.0)
                v_new = jnp.where(is_ice, v_new, 0.0)
            u_next[j, rows] = u_new
            v_next[j, rows] = v_new

    for j in range(TPD):
        ice[j, middle, :] = jnp.ones((TS, LANES), jnp.float32)

    def sweep(*state):
        @pl.loop(0, TPD)
        def _(j):
            viscosity(*state[:2], j, in_tile)

        viscosity(*state[:2], TPD, in_columns)

        @pl.loop(0, TPD)
        def _(j):
            relax(*state, j, in_tile)

        relax(*state, TPD, in_columns)

    @pl.loop(0, SWEEPS // 2)
    def _(_):
        sweep(u, v, u_other, v_other)
        sweep(u_other, v_other, u, v)

    def given(j):
        refs = (vel_ref.at[0, j], vel_ref.at[1, j], next_ref.at[j])
        return [pltpu.make_async_copy(results.at[k, j], ref, out_sems.at[k, j]) for k, ref in enumerate(refs)]

    @pl.loop(0, TPD)
    def _(j):
        part = 64
        back = LANES - MARGIN - 2 * MARGIN * j

        for start in range(TOP, TOP + TS, part):
            rows, under, over = (slice(start + k, start + k + part) for k in (0, -1, 1))
            u_c, u_lx, u_ux = in_tile(u, j, rows)
            h_c, h_lx, h_ux = in_tile(h, j, rows)
            v_c = v[j, rows]
            s_lx, s_ux = 0.5 * (u_lx + u_c), 0.5 * (u_c + u_ux)
            s_ly, s_uy = 0.5 * (v[j, under] + v_c), 0.5 * (v_c + v[j, over])
            flux_lx = jnp.maximum(s_lx, 0.0) * h_lx + jnp.minimum(s_lx, 0.0) * h_c
            flux_ux = jnp.maximum(s_ux, 0.0) * h_c + jnp.minimum(s_ux, 0.0) * h_ux
            flux_ly = jnp.maximum(s_ly, 0.0) * h[j, under] + jnp.minimum(s_ly, 0.0) * h_c
            flux_uy = jnp.maximum(s_uy, 0.0) * h_c + jnp.minimum(s_uy, 0.0) * h[j, over]
            h_next = h_c - TIME_STEP * (flux_ux - flux_lx + flux_uy - flux_ly)
            for k, value in enumerate((u_c, v_c, h_next)):
                results[k, j, start - TOP : start - TOP + part, :] = pltpu.roll(value, back, 1)
        for copy in given(j):
            copy.start()

    for j in range(TPD):
        for copy in given(j):
            copy.wait()


def shards(slots, thickness, driving, friction, velocity_start, row_lengths):
    f32 = jnp.float32
    vmem = pl.BlockSpec(memory_space=pltpu.VMEM)
    smem = pl.BlockSpec(memory_space=pltpu.SMEM)
    anywhere = pl.BlockSpec(memory_space=pl.ANY)
    params = pltpu.CompilerParams(vmem_limit_bytes=VMEM_LIMIT)
    strips_shape = jax.ShapeDtypeStruct((TPD, STRIP, LANES), f32)
    columns_shape = jax.ShapeDtypeStruct((TS, LANES), f32)
    field_shape = jax.ShapeDtypeStruct((TPD + 1, ROWS, LANES), f32)
    pack_shape = jax.ShapeDtypeStruct((FULL_PACK, LANES), f32)
    rows = row_lengths.shape[0]
    cost = pl.CostEstimate(flops=4_000_000, bytes_accessed=4_000_000, transcendentals=0)
    given = (thickness, driving, friction, velocity_start)

    with jax.named_scope("sent_strips"):
        sent_bottom, sent_top = pl.pallas_call(
            sent_strips_kernel,
            out_shape=(strips_shape, strips_shape),
            in_specs=[anywhere] * 4,
            out_specs=(vmem,) * 2,
            scratch_shapes=[
                pltpu.VMEM((2, 6, TPD, 2 * SECTION, LANES), f32),
                pltpu.SemaphoreType.DMA((2, 6)),
            ],
            compiler_params=pltpu.CompilerParams(vmem_limit_bytes=FIRST_VMEM_LIMIT),
        )(*given)

    with jax.named_scope("own_strips"):
        bottom, top, right, left = pl.pallas_call(
            own_strips_kernel,
            out_shape=(strips_shape, strips_shape, columns_shape, columns_shape),
            in_specs=[vmem] * 4,
            out_specs=(vmem,) * 4,
            cost_estimate=cost,
            compiler_params=params,
        )(*given)

    with jax.named_scope("plan"):
        plan = pl.pallas_call(
            functools.partial(plan_kernel, slots),
            out_shape=jax.ShapeDtypeStruct((PLAN,), jnp.int32),
            in_specs=[smem],
            out_specs=anywhere,
            scratch_shapes=[pltpu.SMEM((PLAN,), jnp.int32), pltpu.SMEM((rows,), jnp.int32), pltpu.SemaphoreType.DMA],
            cost_estimate=cost,
        )(row_lengths)

    with jax.named_scope("own_fields"):
        fields = pl.pallas_call(
            own_fields_kernel,
            out_shape=(field_shape,) * 6,
            in_specs=[vmem] * 4,
            out_specs=(vmem,) * 6,
            cost_estimate=cost,
            compiler_params=params,
        )(*given)

    with jax.named_scope("strides"):
        bottoms = [bottom] + [cyclic_shift(sent_bottom, STRIDE * a) for a in range(1, HOPS)]
        tops = [top] + [cyclic_shift(sent_top, -STRIDE * a) for a in range(1, HOPS)]

    with jax.named_scope("route"):
        back, local, ahead = pl.pallas_call(
            route_kernel,
            out_shape=(pack_shape, jax.ShapeDtypeStruct((PACK, LANES), f32), pack_shape),
            in_specs=[anywhere] + [vmem] * (2 * HOPS + 2),
            out_specs=(vmem,) * 3,
            scratch_shapes=[pltpu.SMEM((PLAN,), jnp.int32), pltpu.SemaphoreType.DMA],
            compiler_params=params,
        )(plan, *bottoms, *tops, right, left)

    with jax.named_scope("last_step"):
        back = cyclic_shift(back, -1)
        ahead = cyclic_shift(ahead, 1)

    with jax.named_scope("sweeps"):
        field = pltpu.VMEM(field_shape.shape, f32)
        velocity, thickness_next, *_ = pl.pallas_call(
            sweeps_kernel,
            out_shape=(
                jax.ShapeDtypeStruct(velocity_start.shape, f32),
                jax.ShapeDtypeStruct(thickness.shape, f32),
            ) + (field_shape,) * 6,
            in_specs=[smem] + [anywhere] * 3 + [vmem] * 6,
            out_specs=(anywhere, anywhere) + (vmem,) * 6,
            input_output_aliases={4 + k: 2 + k for k in range(6)},
            scratch_shapes=[
                *[field] * 8,
                pltpu.VMEM((3, TPD, TS, LANES), f32),
                pltpu.VMEM((3, FULL_PACK, LANES), f32),
                pltpu.SemaphoreType.DMA((3,)),
                pltpu.SemaphoreType.DMA((3, TPD)),
            ],
            compiler_params=params,
        )(plan, ahead, local, back, *fields)
    return velocity, thickness_next


def solution(mesh):
    in_specs = (
        P("ta", None, None),
        P(None, "ta", None, None),
        P(("ma", "ta"), None, None),
        P(None, "ta", None, None),
        P(),
    )
    out_specs = (P(None, ("ma", "ta"), None, None), P(("ma", "ta"), None, None))
    slots = TPD * mesh.shape["ta"]
    return jax.shard_map(
        functools.partial(shards, slots), mesh=mesh, in_specs=in_specs, out_specs=out_specs, check_vma=False
    )
```

```python
import functools

import jax
import jax.numpy as jnp
from jax import lax
from jax.experimental import pallas as pl
from jax.experimental.pallas import tpu as pltpu
from jax.sharding import PartitionSpec as P


GC = 48
SWEEPS = 4
STRAIN_EPSILON = 0.01
TIME_STEP = 0.1

TS = 128
LANES = 128
TPD = 4
SECTION = 8
STRIP = 6 * SECTION
TOP = 16
ROWS = TS + 2 * TOP
MARGIN = 16
STRIDE = 3
HOPS = 5
MAIN_BLOCKS = 2 * TPD
PACK = (MAIN_BLOCKS + 2) * STRIP
GROUP = 10
HALF = TS // 2
FULL_PACK = PACK + HALF
VMEM_LIMIT = 40 * 1024 * 1024
FIRST_VMEM_LIMIT = 60 * 1024 * 1024
ROUTE = 3 * TPD * 2 * 3
WHICH = ROUTE
BITS = WHICH + 2 * TPD
PLAN = 128


def cyclic_shift(value, steps):
    count = lax.axis_size("ta")
    return lax.ppermute(value, "ta", [(i, (i + steps) % count) for i in range(count)])


def fill_row_ends(len_ref, ends_ref):
    total = jnp.int32(0)
    ends = []
    for r in range(len_ref.shape[0]):
        total = total + len_ref[r]
        ends_ref[r] = total
        ends.append(total)
    return ends


class Tile:
    def __init__(self, len_ref, ends_ref, ends, slot, slots):
        rows = len_ref.shape[0]
        row = jnp.int32(0)
        for end in ends:
            row = row + jnp.where(end <= slot, 1, 0)
        self.slot = slot
        self.real = (slot >= 0) & (slot < slots)
        row = jnp.minimum(row, rows - 1)
        self.length = len_ref[row]
        self.above = jnp.where(row >= 1, len_ref[jnp.maximum(row - 1, 0)], 0)
        self.below = jnp.where(row < rows - 1, len_ref[jnp.minimum(row + 1, rows - 1)], 0)
        self.column = GC + slot - ends_ref[row]

    def side(self, down, step):
        column = self.column + step
        length = self.below if down else self.above
        there = self.real & (column < GC) & (column >= GC - length)
        slot = self.slot + (self.below if down else -self.length) + step
        return there, slot

    def lower_x(self):
        return self.real & (self.column > GC - self.length)

    def upper_x(self):
        return self.real & (self.column < GC - 1)


def hop(device, slot, down):
    owner = slot >> 2
    q = jnp.maximum((owner - device) if down else (device - owner), 0)
    a = jnp.minimum(((q + 1) * 11) >> 5, HOPS - 1)
    b = q - STRIDE * a
    return a, (-b if down else b)


def field_refs(h_ref, d_ref, f_ref, v_ref):
    return [v_ref.at[0], v_ref.at[1], h_ref, d_ref.at[0], d_ref.at[1], f_ref]


def put_strips(ends, bottom_ref, top_ref):
    row = lax.broadcasted_iota(jnp.int32, (SECTION, LANES), 0)
    for t in range(TPD):
        for k in range(6):
            last = ends(k, t, slice(TS - SECTION, TS))
            first = ends(k, t, slice(0, SECTION))
            if k in (3, 4):
                last = jnp.where(row == 0, ends(k - 3, t, slice(TS - SECTION - 1, TS - SECTION)), last)
                first = jnp.where(row == SECTION - 1, ends(k - 3, t, slice(SECTION, SECTION + 1)), first)
            bottom_ref[t, k * SECTION : (k + 1) * SECTION, :] = last
            top_ref[t, k * SECTION : (k + 1) * SECTION, :] = first


def sent_strips_kernel(h_ref, d_ref, f_ref, v_ref, bottom_ref, top_ref, held, sems):
    copies = []
    for k, ref in enumerate(field_refs(h_ref, d_ref, f_ref, v_ref)):
        copies += [
            pltpu.make_async_copy(ref.at[:, pl.ds(0, 2 * SECTION)], held.at[0, k], sems.at[0, k]),
            pltpu.make_async_copy(ref.at[:, pl.ds(TS - 2 * SECTION, 2 * SECTION)], held.at[1, k], sems.at[1, k]),
        ]
    for copy in copies:
        copy.start()
    for copy in copies:
        copy.wait()

    def ends(k, t, rows):
        if rows.start < 2 * SECTION:
            return held[0, k, t, rows, :]
        return held[1, k, t, rows.start - TS + 2 * SECTION : rows.stop - TS + 2 * SECTION, :]

    put_strips(ends, bottom_ref, top_ref)


def own_strips_kernel(h_ref, d_ref, f_ref, v_ref, bottom_ref, top_ref, right_ref, left_ref):
    fields = field_refs(h_ref, d_ref, f_ref, v_ref)
    put_strips(lambda k, t, rows: fields[k][t, rows, :], bottom_ref, top_ref)
    lane = lax.broadcasted_iota(jnp.int32, (HALF, LANES), 1)
    right = left = jnp.zeros((HALF, LANES), jnp.float32)
    for k, field in enumerate(fields):
        for half in (0, 1):
            start = half * HALF + k * GROUP
            here = (lane >= start) & (lane < start + GROUP)
            rows = slice(half * HALF, (half + 1) * HALF)
            right = jnp.where(here, pltpu.roll(field[TPD - 1, rows, :], (start + GROUP) % LANES, 1), right)
            left = jnp.where(here, pltpu.roll(field[0, rows, :], start, 1) if start else field[0, rows, :], left)
    right_ref[...] = right
    left_ref[...] = left


def plan_kernel(slots, len_ref, out_ref, plan_ref, ends_ref, sem):
    ends = fill_row_ends(len_ref, ends_ref)
    me, count = lax.axis_index("ta"), slots // TPD
    for step in (-1, 0, 1):
        device = lax.rem(me + step + count, count)
        tiles = [Tile(len_ref, ends_ref, ends, device * TPD + j, slots) for j in range(TPD)]
        for j, tile in enumerate(tiles):
            for down in (0, 1):
                for across in (-1, 0, 1):
                    there, slot = tile.side(down, across)
                    a, shift = hop(device, slot, down)
                    entry = (((step + 1) * TPD + j) * 2 + down) * 3 + across + 1
                    plan_ref[0, entry] = jnp.where(there & (shift == step), TPD * a + (slot & 3), -1)
                    if step == 0 and across == 0:
                        plan_ref[0, WHICH + down * TPD + j] = jnp.where(there, shift + 1, -1)
        if step == 0:
            for down in (0, 1):
                plan_ref[0, BITS + down] = flag_bits([t.side(down, k)[0] for t in tiles for k in (-1, 1)])
            plan_ref[0, BITS + 2] = flag_bits([flag for t in tiles for flag in (t.lower_x(), t.upper_x())])
    for unused in range(BITS + 3, PLAN):
        plan_ref[0, unused] = 0
    copy = pltpu.make_async_copy(plan_ref, out_ref, sem)
    copy.start()
    copy.wait()


def flag_bits(flags):
    bits = jnp.int32(0)
    for k, flag in enumerate(flags):
        bits = bits + jnp.where(flag, 1 << k, 0)
    return bits


def own_fields_kernel(h_ref, d_ref, f_ref, v_ref, *outs):
    group = lax.broadcasted_iota(jnp.int32, (TS, LANES), 1) >> 4
    middle = slice(TOP, TOP + TS)
    for ref, out in zip(field_refs(h_ref, d_ref, f_ref, v_ref), outs):
        edges = None
        for j in range(TPD):
            tile = pltpu.roll(ref[j], 2 * MARGIN * j + MARGIN, 1)
            out[j, middle, :] = tile
            edges = tile if j == 0 else jnp.where((group >> 1) == j, tile, edges)
        lower, upper = pltpu.roll(edges, 2 * MARGIN, 1), pltpu.roll(edges, LANES - 2 * MARGIN, 1)
        out[TPD, middle, :] = jnp.where((group & 1) == 0, lower, upper)


def route_kernel(given_plan, *refs):
    given = refs[: 2 * HOPS]
    right_ref, left_ref = refs[2 * HOPS : 2 * HOPS + 2]
    outs = refs[2 * HOPS + 2 : 2 * HOPS + 5]
    plan_ref, sem = refs[2 * HOPS + 5 :]
    copy = pltpu.make_async_copy(given_plan, plan_ref, sem)
    copy.start()
    outs[0][PACK:, :] = left_ref[...]
    outs[2][PACK:, :] = right_ref[...]
    for out in outs:
        out[MAIN_BLOCKS * STRIP : PACK, :] = jnp.zeros((2 * STRIP, LANES), jnp.float32)
    lane = lax.broadcasted_iota(jnp.int32, (STRIP, LANES), 1)
    copy.wait()
    for step, out in enumerate(outs):
        for down in (0, 1):
            for across in (-1, 0, 1):

                @pl.loop(0, TPD)
                def _(j, step=step, out=out, down=down, across=across):
                    source = plan_ref[0, ((step * TPD + j) * 2 + down) * 3 + across + 1]

                    @pl.when(source >= 0)
                    def _():
                        for a in range(HOPS):

                            @pl.when((source >> 2) == a)
                            def _():
                                strip = given[down * HOPS + a][source & 3]
                                moved = pltpu.roll(strip, 2 * MARGIN * j + MARGIN, 1)
                                if across == 0:
                                    out[pl.ds(pl.multiple_of((down * TPD + j) * STRIP, 8), STRIP), :] = moved
                                else:
                                    rows = slice((MAIN_BLOCKS + down) * STRIP, (MAIN_BLOCKS + down + 1) * STRIP)
                                    here = (lane >> 4) == 2 * j + (across + 1) // 2
                                    out[rows, :] = jnp.where(here, moved, out[rows, :])


def group_mask(bits, shape):
    group = lax.broadcasted_iota(jnp.int32, shape, 1) >> 4
    return ((jnp.full(shape, bits) >> group) & 1) == 1


def sweeps_kernel(given_plan, ahead_ref, local_ref, back_ref, *refs):
    vel_ref, next_ref, u, v, h, d0, d1, f = refs[6:14]
    u_other, v_other, w, ice, u_low, u_high, v_low, v_high, results, out_sems, plan_ref, sem = refs[14:]
    plan_copy = pltpu.make_async_copy(given_plan, plan_ref, sem)
    plan_copy.start()
    packs = (back_ref, local_ref, ahead_ref)
    zero = jnp.zeros((SECTION, LANES), jnp.float32)
    one = jnp.ones((SECTION, LANES), jnp.float32)
    for block in range(TPD + 1):
        for start in (0, ROWS - SECTION):
            rows = slice(start, start + SECTION)
            u[block, rows, :] = zero
            v[block, rows, :] = zero
            w[block, rows, :] = zero
    for j in range(TPD):
        ice[j, TOP : TOP + TS, :] = jnp.ones((TS, LANES), jnp.float32)
    plan_copy.wait()

    targets = (u, v, h, d0, d1, f)
    for down in (0, 1):
        start = TOP + TS if down else TOP - SECTION
        rows = slice(start, start + SECTION)
        deep = SECTION - 1 if down else 0
        far = start + SECTION if down else start - 1

        def put(j, parts, mask=None, rows=rows, deep=deep, far=far):
            for k, target in enumerate(targets):
                target[j, rows, :] = parts[k] if mask is None else jnp.where(mask, parts[k], one if k == 5 else zero)
            for k in (0, 1):
                line = parts[3 + k] if mask is None else jnp.where(mask, parts[3 + k], zero)
                targets[k][j, far : far + 1, :] = line[deep : deep + 1, :]

        def sections(pack, block):
            return [pack[block * STRIP + k * SECTION : block * STRIP + (k + 1) * SECTION, :] for k in range(6)]

        for j in range(TPD):
            which = plan_ref[0, WHICH + down * TPD + j]
            for index, pack in enumerate(packs):

                @pl.when(which == index)
                def _(j=j, pack=pack, down=down, put=put, sections=sections, rows=rows):
                    put(j, sections(pack, down * TPD + j))
                    ice[j, rows, :] = one

            @pl.when(which < 0)
            def _(j=j, put=put, rows=rows):
                put(j, [zero] * 5 + [one])
                ice[j, rows, :] = zero

        mask = group_mask(plan_ref[0, BITS + down], (SECTION, LANES))
        parts = [sum(part) for part in zip(*[sections(pack, MAIN_BLOCKS + down) for pack in packs])]
        put(TPD, parts, mask)
        ice[TPD, rows, :] = jnp.where(mask, one, zero)

    mask = group_mask(plan_ref[0, BITS + 2], (TS, LANES))
    group = lax.broadcasted_iota(jnp.int32, (TS, LANES), 1) >> 4
    middle = slice(TOP, TOP + TS)
    ice[TPD, middle, :] = jnp.where(mask, 1.0, 0.0)
    group = group[:HALF]
    for k, target in enumerate(targets):
        for half in (0, 1):
            start = half * HALF + k * GROUP
            rows = slice(TOP + half * HALF, TOP + (half + 1) * HALF)
            before = pltpu.roll(ahead_ref[PACK:, :], (MARGIN - GROUP - start) % LANES, 1)
            after = pltpu.roll(back_ref[PACK:, :], (LANES - MARGIN - start) % LANES, 1)
            beside = jnp.where(group == 0, before, target[TPD, rows, :])
            beside = jnp.where(group == 2 * TPD - 1, after, beside)
            target[TPD, rows, :] = jnp.where(mask[:HALF], beside, 1.0 if k == 5 else 0.0)

    chunk = 48
    first_row, last_row = TOP - SECTION, TOP + TS + SECTION

    def in_tile(ref, j, rows):
        centre, edge = ref[j, rows], ref[TPD, rows]
        lane = lax.broadcasted_iota(jnp.int32, centre.shape, 1)
        high_side = 2 * MARGIN * j + MARGIN
        lower = pltpu.roll(jnp.where(lane == high_side - 1, edge, centre), 1, 1)
        upper = pltpu.roll(jnp.where(lane == high_side, edge, centre), LANES - 1, 1)
        return centre, lower, upper

    def in_columns(ref, j, rows):
        centre, edge = ref[TPD, rows], ref[0, rows]
        lane = lax.broadcasted_iota(jnp.int32, centre.shape, 1)
        for t in range(1, TPD):
            edge = jnp.where((lane >> 5) == t, ref[t, rows], edge)
        within = lane & (2 * MARGIN - 1)
        lower = pltpu.roll(jnp.where(within == MARGIN - 1, edge, centre), 1, 1)
        upper = pltpu.roll(jnp.where(within == MARGIN, edge, centre), LANES - 1, 1)
        return centre, lower, upper

    def viscosity(u, v, j, beside):
        for start in range(first_row, last_row, chunk):
            rows, under, over = (slice(start + k, start + k + chunk) for k in (0, -1, 1))
            _, u_lx, u_ux = beside(u, j, rows)
            _, v_lx, v_ux = beside(v, j, rows)
            u_low[j, rows], u_high[j, rows] = u_lx, u_ux
            v_low[j, rows], v_high[j, rows] = v_lx, v_ux
            ux = u_ux - u_lx
            vy = v[j, over] - v[j, under]
            shear = (u[j, over] - u[j, under]) + (v_ux - v_lx)
            strain = 0.25 * (ux * ux + vy * vy + ux * vy + 0.25 * shear * shear) + STRAIN_EPSILON
            w[j, rows] = (0.25 * h[j, rows]) * jnp.exp(jnp.log(strain) * (-1.0 / 3.0))

    def quotient(top, bottom):
        guess = pl.reciprocal(bottom, approx=True)
        return top * (guess * (2.0 - bottom * guess))

    def relax(u, v, u_next, v_next, j, beside):
        for start in range(first_row, last_row, chunk):
            rows, under, over = (slice(start + k, start + k + chunk) for k in (0, -1, 1))
            here, w_lx, w_ux = beside(w, j, rows)
            c_lx, c_ux = here + w_lx, here + w_ux
            c_ly, c_uy = here + w[j, under], here + w[j, over]
            u_lx, u_ux = u_low[j, rows], u_high[j, rows]
            v_lx, v_ux = v_low[j, rows], v_high[j, rows]
            c_x, c_y = c_lx + c_ux, c_ly + c_uy
            drag = f[j, rows]
            u_top = 4.0 * (c_lx * u_lx + c_ux * u_ux) + c_ly * u[j, under] + c_uy * u[j, over] - d0[j, rows]
            v_top = c_lx * v_lx + c_ux * v_ux + 4.0 * (c_ly * v[j, under] + c_uy * v[j, over]) - d1[j, rows]
            u_new = quotient(u_top, 4.0 * c_x + c_y + drag)
            v_new = quotient(v_top, c_x + 4.0 * c_y + drag)
            if beside is in_columns or start == first_row or start + chunk == last_row:
                is_ice = ice[j, rows] > 0.0
                u_new = jnp.where(is_ice, u_new, 0.0)
                v_new = jnp.where(is_ice, v_new, 0.0)
            u_next[j, rows] = u_new
            v_next[j, rows] = v_new

    def sweep(*state):
        @pl.loop(0, TPD)
        def _(j):
            viscosity(*state[:2], j, in_tile)

        viscosity(*state[:2], TPD, in_columns)

        @pl.loop(0, TPD)
        def _(j):
            relax(*state, j, in_tile)

        relax(*state, TPD, in_columns)

    @pl.loop(0, SWEEPS // 2)
    def _(_):
        sweep(u, v, u_other, v_other)
        sweep(u_other, v_other, u, v)

    def given(j):
        refs = (vel_ref.at[0, j], vel_ref.at[1, j], next_ref.at[j])
        return [pltpu.make_async_copy(results.at[k, j], ref, out_sems.at[k, j]) for k, ref in enumerate(refs)]

    @pl.loop(0, TPD)
    def _(j):
        part = 64
        back = LANES - MARGIN - 2 * MARGIN * j

        for start in range(TOP, TOP + TS, part):
            rows, under, over = (slice(start + k, start + k + part) for k in (0, -1, 1))
            u_c, u_lx, u_ux = in_tile(u, j, rows)
            h_c, h_lx, h_ux = in_tile(h, j, rows)
            v_c = v[j, rows]
            s_lx, s_ux = 0.5 * (u_lx + u_c), 0.5 * (u_c + u_ux)
            s_ly, s_uy = 0.5 * (v[j, under] + v_c), 0.5 * (v_c + v[j, over])
            flux_lx = jnp.maximum(s_lx, 0.0) * h_lx + jnp.minimum(s_lx, 0.0) * h_c
            flux_ux = jnp.maximum(s_ux, 0.0) * h_c + jnp.minimum(s_ux, 0.0) * h_ux
            flux_ly = jnp.maximum(s_ly, 0.0) * h[j, under] + jnp.minimum(s_ly, 0.0) * h_c
            flux_uy = jnp.maximum(s_uy, 0.0) * h_c + jnp.minimum(s_uy, 0.0) * h[j, over]
            h_next = h_c - TIME_STEP * (flux_ux - flux_lx + flux_uy - flux_ly)
            for k, value in enumerate((u_c, v_c, h_next)):
                results[k, j, start - TOP : start - TOP + part, :] = pltpu.roll(value, back, 1)
        for copy in given(j):
            copy.start()

    for j in range(TPD):
        for copy in given(j):
            copy.wait()


def shards(slots, thickness, driving, friction, velocity_start, row_lengths):
    f32 = jnp.float32
    vmem = pl.BlockSpec(memory_space=pltpu.VMEM)
    smem = pl.BlockSpec(memory_space=pltpu.SMEM)
    anywhere = pl.BlockSpec(memory_space=pl.ANY)
    params = pltpu.CompilerParams(vmem_limit_bytes=VMEM_LIMIT)
    strips_shape = jax.ShapeDtypeStruct((TPD, STRIP, LANES), f32)
    columns_shape = jax.ShapeDtypeStruct((HALF, LANES), f32)
    field_shape = jax.ShapeDtypeStruct((TPD + 1, ROWS, LANES), f32)
    pack_shape = jax.ShapeDtypeStruct((FULL_PACK, LANES), f32)
    rows = row_lengths.shape[0]
    cost = pl.CostEstimate(flops=4_000_000, bytes_accessed=4_000_000, transcendentals=0)
    given = (thickness, driving, friction, velocity_start)

    with jax.named_scope("sent_strips"):
        sent_bottom, sent_top = pl.pallas_call(
            sent_strips_kernel,
            out_shape=(strips_shape, strips_shape),
            in_specs=[anywhere] * 4,
            out_specs=(vmem,) * 2,
            scratch_shapes=[
                pltpu.VMEM((2, 6, TPD, 2 * SECTION, LANES), f32),
                pltpu.SemaphoreType.DMA((2, 6)),
            ],
            compiler_params=pltpu.CompilerParams(vmem_limit_bytes=FIRST_VMEM_LIMIT),
        )(*given)

    with jax.named_scope("own_strips"):
        bottom, top, right, left = pl.pallas_call(
            own_strips_kernel,
            out_shape=(strips_shape, strips_shape, columns_shape, columns_shape),
            in_specs=[vmem] * 4,
            out_specs=(vmem,) * 4,
            cost_estimate=cost,
            compiler_params=params,
        )(*given)

    with jax.named_scope("plan"):
        plan = pl.pallas_call(
            functools.partial(plan_kernel, slots),
            out_shape=jax.ShapeDtypeStruct((1, PLAN), jnp.int32),
            in_specs=[smem],
            out_specs=vmem,
            scratch_shapes=[pltpu.SMEM((1, PLAN), jnp.int32), pltpu.SMEM((rows,), jnp.int32), pltpu.SemaphoreType.DMA],
            cost_estimate=cost,
            compiler_params=params,
        )(row_lengths)

    with jax.named_scope("own_fields"):
        fields = pl.pallas_call(
            own_fields_kernel,
            out_shape=(field_shape,) * 6,
            in_specs=[vmem] * 4,
            out_specs=(vmem,) * 6,
            cost_estimate=cost,
            compiler_params=params,
        )(*given)

    with jax.named_scope("strides"):
        bottoms = [bottom] + [cyclic_shift(sent_bottom, STRIDE * a) for a in range(1, HOPS)]
        tops = [top] + [cyclic_shift(sent_top, -STRIDE * a) for a in range(1, HOPS)]

    with jax.named_scope("route"):
        back, local, ahead = pl.pallas_call(
            route_kernel,
            out_shape=(pack_shape, jax.ShapeDtypeStruct((PACK, LANES), f32), pack_shape),
            in_specs=[vmem] * (2 * HOPS + 3),
            out_specs=(vmem,) * 3,
            scratch_shapes=[pltpu.SMEM((1, PLAN), jnp.int32), pltpu.SemaphoreType.DMA],
            compiler_params=params,
        )(plan, *bottoms, *tops, right, left)

    with jax.named_scope("last_step"):
        back = cyclic_shift(back, -1)
        ahead = cyclic_shift(ahead, 1)

    with jax.named_scope("sweeps"):
        field = pltpu.VMEM(field_shape.shape, f32)
        velocity, thickness_next, *_ = pl.pallas_call(
            sweeps_kernel,
            out_shape=(
                jax.ShapeDtypeStruct(velocity_start.shape, f32),
                jax.ShapeDtypeStruct(thickness.shape, f32),
            ) + (field_shape,) * 6,
            in_specs=[vmem] * 10,
            out_specs=(anywhere, anywhere) + (vmem,) * 6,
            input_output_aliases={4 + k: 2 + k for k in range(6)},
            scratch_shapes=[
                *[field] * 8,
                pltpu.VMEM((3, TPD, TS, LANES), f32),
                pltpu.SemaphoreType.DMA((3, TPD)),
                pltpu.SMEM((1, PLAN), jnp.int32),
                pltpu.SemaphoreType.DMA,
            ],
            compiler_params=params,
        )(plan, ahead, local, back, *fields)
    return velocity, thickness_next


def solution(mesh):
    in_specs = (
        P("ta", None, None),
        P(None, "ta", None, None),
        P(("ma", "ta"), None, None),
        P(None, "ta", None, None),
        P(),
    )
    out_specs = (P(None, ("ma", "ta"), None, None), P(("ma", "ta"), None, None))
    slots = TPD * mesh.shape["ta"]
    return jax.shard_map(
        functools.partial(shards, slots), mesh=mesh, in_specs=in_specs, out_specs=out_specs, check_vma=False
    )
```

```python
import functools

import jax
import jax.numpy as jnp
from jax import lax
from jax.experimental import pallas as pl
from jax.experimental.pallas import tpu as pltpu
from jax.sharding import PartitionSpec as P


GC = 48
SWEEPS = 4
STRAIN_EPSILON = 0.01
TIME_STEP = 0.1

TS = 128
LANES = 128
TPD = 4
SECTION = 8
STRIP = 6 * SECTION
TOP = 16
ROWS = TS + 2 * TOP
MARGIN = 16
STRIDE = 3
HOPS = 5
MAIN_BLOCKS = 2 * TPD
PACK = (MAIN_BLOCKS + 1) * STRIP
CORNER = 8
GROUP = 10
HALF = TS // 2
FULL_PACK = PACK + HALF
VMEM_LIMIT = 40 * 1024 * 1024
FIRST_VMEM_LIMIT = 60 * 1024 * 1024
ROUTE = 3 * TPD * 2 * 3
WHICH = ROUTE
BITS = WHICH + 2 * TPD
PLAN = 128


def cyclic_shift(value, steps):
    count = lax.axis_size("ta")
    return lax.ppermute(value, "ta", [(i, (i + steps) % count) for i in range(count)])


def fill_row_ends(len_ref, ends_ref):
    total = jnp.int32(0)
    ends = []
    for r in range(len_ref.shape[0]):
        total = total + len_ref[r]
        ends_ref[r] = total
        ends.append(total)
    return ends


class Tile:
    def __init__(self, len_ref, ends_ref, ends, slot, slots):
        rows = len_ref.shape[0]
        row = jnp.int32(0)
        for end in ends:
            row = row + jnp.where(end <= slot, 1, 0)
        self.slot = slot
        self.real = (slot >= 0) & (slot < slots)
        row = jnp.minimum(row, rows - 1)
        self.length = len_ref[row]
        self.above = jnp.where(row >= 1, len_ref[jnp.maximum(row - 1, 0)], 0)
        self.below = jnp.where(row < rows - 1, len_ref[jnp.minimum(row + 1, rows - 1)], 0)
        self.column = GC + slot - ends_ref[row]

    def side(self, down, step):
        column = self.column + step
        length = self.below if down else self.above
        there = self.real & (column < GC) & (column >= GC - length)
        slot = self.slot + (self.below if down else -self.length) + step
        return there, slot

    def lower_x(self):
        return self.real & (self.column > GC - self.length)

    def upper_x(self):
        return self.real & (self.column < GC - 1)


def hop(device, slot, down):
    owner = slot >> 2
    q = jnp.maximum((owner - device) if down else (device - owner), 0)
    a = jnp.minimum(((q + 1) * 11) >> 5, HOPS - 1)
    b = q - STRIDE * a
    return a, (-b if down else b)


def field_refs(h_ref, d_ref, f_ref, v_ref):
    return [v_ref.at[0], v_ref.at[1], h_ref, d_ref.at[0], d_ref.at[1], f_ref]


def put_strips(ends, bottom_ref, top_ref):
    row = lax.broadcasted_iota(jnp.int32, (SECTION, LANES), 0)
    for t in range(TPD):
        for k in range(6):
            last = ends(k, t, slice(TS - SECTION, TS))
            first = ends(k, t, slice(0, SECTION))
            if k in (3, 4):
                last = jnp.where(row == 0, ends(k - 3, t, slice(TS - SECTION - 1, TS - SECTION)), last)
                first = jnp.where(row == SECTION - 1, ends(k - 3, t, slice(SECTION, SECTION + 1)), first)
            bottom_ref[t, k * SECTION : (k + 1) * SECTION, :] = last
            top_ref[t, k * SECTION : (k + 1) * SECTION, :] = first


def sent_strips_kernel(h_ref, d_ref, f_ref, v_ref, bottom_ref, top_ref, held, sems):
    copies = []
    for k, ref in enumerate(field_refs(h_ref, d_ref, f_ref, v_ref)):
        copies += [
            pltpu.make_async_copy(ref.at[:, pl.ds(0, 2 * SECTION)], held.at[0, k], sems.at[0, k]),
            pltpu.make_async_copy(ref.at[:, pl.ds(TS - 2 * SECTION, 2 * SECTION)], held.at[1, k], sems.at[1, k]),
        ]
    for copy in copies:
        copy.start()
    for copy in copies:
        copy.wait()

    def ends(k, t, rows):
        if rows.start < 2 * SECTION:
            return held[0, k, t, rows, :]
        return held[1, k, t, rows.start - TS + 2 * SECTION : rows.stop - TS + 2 * SECTION, :]

    put_strips(ends, bottom_ref, top_ref)


def own_strips_kernel(h_ref, d_ref, f_ref, v_ref, bottom_ref, top_ref, right_ref, left_ref):
    fields = field_refs(h_ref, d_ref, f_ref, v_ref)
    put_strips(lambda k, t, rows: fields[k][t, rows, :], bottom_ref, top_ref)
    lane = lax.broadcasted_iota(jnp.int32, (HALF, LANES), 1)
    right = left = jnp.zeros((HALF, LANES), jnp.float32)
    for k, field in enumerate(fields):
        for half in (0, 1):
            start = half * HALF + k * GROUP
            here = (lane >= start) & (lane < start + GROUP)
            rows = slice(half * HALF, (half + 1) * HALF)
            right = jnp.where(here, pltpu.roll(field[TPD - 1, rows, :], (start + GROUP) % LANES, 1), right)
            left = jnp.where(here, pltpu.roll(field[0, rows, :], start, 1) if start else field[0, rows, :], left)
    right_ref[...] = right
    left_ref[...] = left


def plan_kernel(slots, len_ref, out_ref, plan_ref, ends_ref, sem):
    ends = fill_row_ends(len_ref, ends_ref)
    me, count = lax.axis_index("ta"), slots // TPD
    for step in (-1, 0, 1):
        device = lax.rem(me + step + count, count)
        tiles = [Tile(len_ref, ends_ref, ends, device * TPD + j, slots) for j in range(TPD)]
        for j, tile in enumerate(tiles):
            for down in (0, 1):
                for across in (-1, 0, 1):
                    there, slot = tile.side(down, across)
                    a, shift = hop(device, slot, down)
                    entry = (((step + 1) * TPD + j) * 2 + down) * 3 + across + 1
                    plan_ref[0, entry] = jnp.where(there & (shift == step), TPD * a + (slot & 3), -1)
                    if step == 0 and across == 0:
                        plan_ref[0, WHICH + down * TPD + j] = jnp.where(there, shift + 1, -1)
        if step == 0:
            for down in (0, 1):
                plan_ref[0, BITS + down] = flag_bits([t.side(down, k)[0] for t in tiles for k in (-1, 1)])
            plan_ref[0, BITS + 2] = flag_bits([flag for t in tiles for flag in (t.lower_x(), t.upper_x())])
    for unused in range(BITS + 3, PLAN):
        plan_ref[0, unused] = 0
    copy = pltpu.make_async_copy(plan_ref, out_ref, sem)
    copy.start()
    copy.wait()


def flag_bits(flags):
    bits = jnp.int32(0)
    for k, flag in enumerate(flags):
        bits = bits + jnp.where(flag, 1 << k, 0)
    return bits


def own_fields_kernel(h_ref, d_ref, f_ref, v_ref, *outs):
    group = lax.broadcasted_iota(jnp.int32, (TS, LANES), 1) >> 4
    middle = slice(TOP, TOP + TS)
    for ref, out in zip(field_refs(h_ref, d_ref, f_ref, v_ref), outs):
        edges = None
        for j in range(TPD):
            tile = pltpu.roll(ref[j], 2 * MARGIN * j + MARGIN, 1)
            out[j, middle, :] = tile
            edges = tile if j == 0 else jnp.where((group >> 1) == j, tile, edges)
        lower, upper = pltpu.roll(edges, 2 * MARGIN, 1), pltpu.roll(edges, LANES - 2 * MARGIN, 1)
        out[TPD, middle, :] = jnp.where((group & 1) == 0, lower, upper)


def route_kernel(given_plan, *refs):
    given = refs[: 2 * HOPS]
    right_ref, left_ref = refs[2 * HOPS : 2 * HOPS + 2]
    outs = refs[2 * HOPS + 2 : 2 * HOPS + 5]
    plan_ref, sem = refs[2 * HOPS + 5 :]
    copy = pltpu.make_async_copy(given_plan, plan_ref, sem)
    copy.start()
    outs[0][PACK:, :] = left_ref[...]
    outs[2][PACK:, :] = right_ref[...]
    for out in outs:
        out[MAIN_BLOCKS * STRIP : PACK, :] = jnp.zeros((STRIP, LANES), jnp.float32)
    lane = lax.broadcasted_iota(jnp.int32, (STRIP, LANES), 1)
    copy.wait()
    for step, out in enumerate(outs):
        for down in (0, 1):
            for across in (-1, 0, 1):

                @pl.loop(0, TPD)
                def _(j, step=step, out=out, down=down, across=across):
                    source = plan_ref[0, ((step * TPD + j) * 2 + down) * 3 + across + 1]

                    @pl.when(source >= 0)
                    def _():
                        for a in range(HOPS):

                            @pl.when((source >> 2) == a)
                            def _():
                                strip = given[down * HOPS + a][source & 3]
                                turn = 2 * MARGIN * j + MARGIN + (MARGIN * down if across else 0)
                                moved = pltpu.roll(strip, turn & (LANES - 1), 1)
                                if across == 0:
                                    out[pl.ds(pl.multiple_of((down * TPD + j) * STRIP, 8), STRIP), :] = moved
                                else:
                                    rows = slice(MAIN_BLOCKS * STRIP, PACK)
                                    here = (lane >> 3) == ((4 * j + 1 + (across + 1) // 2 + 2 * down) & 15)
                                    out[rows, :] = jnp.where(here, moved, out[rows, :])


def group_mask(bits, shape):
    group = lax.broadcasted_iota(jnp.int32, shape, 1) >> 4
    return ((jnp.full(shape, bits) >> group) & 1) == 1


def sweeps_kernel(given_plan, ahead_ref, local_ref, back_ref, *refs):
    vel_ref, next_ref, u, v, h, d0, d1, f = refs[6:14]
    u_other, v_other, w, ice, u_low, u_high, v_low, v_high, results, out_sems, plan_ref, sem = refs[14:]
    plan_copy = pltpu.make_async_copy(given_plan, plan_ref, sem)
    plan_copy.start()
    packs = (back_ref, local_ref, ahead_ref)
    zero = jnp.zeros((SECTION, LANES), jnp.float32)
    one = jnp.ones((SECTION, LANES), jnp.float32)
    for block in range(TPD + 1):
        for start in (0, ROWS - SECTION):
            rows = slice(start, start + SECTION)
            u[block, rows, :] = zero
            v[block, rows, :] = zero
            w[block, rows, :] = zero
    for j in range(TPD):
        ice[j, TOP : TOP + TS, :] = jnp.ones((TS, LANES), jnp.float32)
    plan_copy.wait()

    targets = (u, v, h, d0, d1, f)
    for down in (0, 1):
        start = TOP + TS if down else TOP - SECTION
        rows = slice(start, start + SECTION)
        deep = SECTION - 1 if down else 0
        far = start + SECTION if down else start - 1

        def put(j, parts, mask=None, rows=rows, deep=deep, far=far):
            for k, target in enumerate(targets):
                target[j, rows, :] = parts[k] if mask is None else jnp.where(mask, parts[k], one if k == 5 else zero)
            for k in (0, 1):
                line = parts[3 + k] if mask is None else jnp.where(mask, parts[3 + k], zero)
                targets[k][j, far : far + 1, :] = line[deep : deep + 1, :]

        def sections(pack, block):
            return [pack[block * STRIP + k * SECTION : block * STRIP + (k + 1) * SECTION, :] for k in range(6)]

        for j in range(TPD):
            which = plan_ref[0, WHICH + down * TPD + j]
            for index, pack in enumerate(packs):

                @pl.when(which == index)
                def _(j=j, pack=pack, down=down, put=put, sections=sections, rows=rows):
                    put(j, sections(pack, down * TPD + j))
                    ice[j, rows, :] = one

            @pl.when(which < 0)
            def _(j=j, put=put, rows=rows):
                put(j, [zero] * 5 + [one])
                ice[j, rows, :] = zero

        within = lax.broadcasted_iota(jnp.int32, (SECTION, LANES), 1) & (2 * MARGIN - 1)
        near = (within >= MARGIN - CORNER) & (within < MARGIN + CORNER)
        mask = group_mask(plan_ref[0, BITS + down], (SECTION, LANES)) & near
        parts = [sum(part) for part in zip(*[sections(pack, MAIN_BLOCKS) for pack in packs])]
        parts = [pltpu.roll(part, LANES - MARGIN, 1) for part in parts] if down else parts
        put(TPD, parts, mask)
        ice[TPD, rows, :] = jnp.where(mask, one, zero)

    mask = group_mask(plan_ref[0, BITS + 2], (TS, LANES))
    group = lax.broadcasted_iota(jnp.int32, (TS, LANES), 1) >> 4
    middle = slice(TOP, TOP + TS)
    ice[TPD, middle, :] = jnp.where(mask, 1.0, 0.0)
    group = group[:HALF]
    for k, target in enumerate(targets):
        for half in (0, 1):
            start = half * HALF + k * GROUP
            rows = slice(TOP + half * HALF, TOP + (half + 1) * HALF)
            before = pltpu.roll(ahead_ref[PACK:, :], (MARGIN - GROUP - start) % LANES, 1)
            after = pltpu.roll(back_ref[PACK:, :], (LANES - MARGIN - start) % LANES, 1)
            beside = jnp.where(group == 0, before, target[TPD, rows, :])
            beside = jnp.where(group == 2 * TPD - 1, after, beside)
            target[TPD, rows, :] = jnp.where(mask[:HALF], beside, 1.0 if k == 5 else 0.0)

    chunk = 48
    first_row, last_row = TOP - SECTION, TOP + TS + SECTION

    def in_tile(ref, j, rows):
        centre, edge = ref[j, rows], ref[TPD, rows]
        lane = lax.broadcasted_iota(jnp.int32, centre.shape, 1)
        high_side = 2 * MARGIN * j + MARGIN
        lower = pltpu.roll(jnp.where(lane == high_side - 1, edge, centre), 1, 1)
        upper = pltpu.roll(jnp.where(lane == high_side, edge, centre), LANES - 1, 1)
        return centre, lower, upper

    def in_columns(ref, j, rows):
        centre, edge = ref[TPD, rows], ref[0, rows]
        lane = lax.broadcasted_iota(jnp.int32, centre.shape, 1)
        for t in range(1, TPD):
            edge = jnp.where((lane >> 5) == t, ref[t, rows], edge)
        within = lane & (2 * MARGIN - 1)
        lower = pltpu.roll(jnp.where(within == MARGIN - 1, edge, centre), 1, 1)
        upper = pltpu.roll(jnp.where(within == MARGIN, edge, centre), LANES - 1, 1)
        return centre, lower, upper

    def viscosity(u, v, j, beside):
        for start in range(first_row, last_row, chunk):
            rows, under, over = (slice(start + k, start + k + chunk) for k in (0, -1, 1))
            _, u_lx, u_ux = beside(u, j, rows)
            _, v_lx, v_ux = beside(v, j, rows)
            u_low[j, rows], u_high[j, rows] = u_lx, u_ux
            v_low[j, rows], v_high[j, rows] = v_lx, v_ux
            ux = u_ux - u_lx
            vy = v[j, over] - v[j, under]
            shear = (u[j, over] - u[j, under]) + (v_ux - v_lx)
            strain = 0.25 * (ux * ux + vy * vy + ux * vy + 0.25 * shear * shear) + STRAIN_EPSILON
            w[j, rows] = (0.25 * h[j, rows]) * jnp.exp(jnp.log(strain) * (-1.0 / 3.0))

    def quotient(top, bottom):
        guess = pl.reciprocal(bottom, approx=True)
        return top * (guess * (2.0 - bottom * guess))

    def relax(u, v, u_next, v_next, j, beside):
        for start in range(first_row, last_row, chunk):
            rows, under, over = (slice(start + k, start + k + chunk) for k in (0, -1, 1))
            here, w_lx, w_ux = beside(w, j, rows)
            c_lx, c_ux = here + w_lx, here + w_ux
            c_ly, c_uy = here + w[j, under], here + w[j, over]
            u_lx, u_ux = u_low[j, rows], u_high[j, rows]
            v_lx, v_ux = v_low[j, rows], v_high[j, rows]
            c_x, c_y = c_lx + c_ux, c_ly + c_uy
            drag = f[j, rows]
            u_top = 4.0 * (c_lx * u_lx + c_ux * u_ux) + c_ly * u[j, under] + c_uy * u[j, over] - d0[j, rows]
            v_top = c_lx * v_lx + c_ux * v_ux + 4.0 * (c_ly * v[j, under] + c_uy * v[j, over]) - d1[j, rows]
            u_new = quotient(u_top, 4.0 * c_x + c_y + drag)
            v_new = quotient(v_top, c_x + 4.0 * c_y + drag)
            if beside is in_columns or start == first_row or start + chunk == last_row:
                is_ice = ice[j, rows] > 0.0
                u_new = jnp.where(is_ice, u_new, 0.0)
                v_new = jnp.where(is_ice, v_new, 0.0)
            u_next[j, rows] = u_new
            v_next[j, rows] = v_new

    def sweep(*state):
        @pl.loop(0, TPD)
        def _(j):
            viscosity(*state[:2], j, in_tile)

        viscosity(*state[:2], TPD, in_columns)

        @pl.loop(0, TPD)
        def _(j):
            relax(*state, j, in_tile)

        relax(*state, TPD, in_columns)

    @pl.loop(0, SWEEPS // 2)
    def _(_):
        sweep(u, v, u_other, v_other)
        sweep(u_other, v_other, u, v)

    def given(j):
        refs = (vel_ref.at[0, j], vel_ref.at[1, j], next_ref.at[j])
        return [pltpu.make_async_copy(results.at[k, j], ref, out_sems.at[k, j]) for k, ref in enumerate(refs)]

    @pl.loop(0, TPD)
    def _(j):
        part = 64
        back = LANES - MARGIN - 2 * MARGIN * j

        for start in range(TOP, TOP + TS, part):
            rows, under, over = (slice(start + k, start + k + part) for k in (0, -1, 1))
            u_c, u_lx, u_ux = in_tile(u, j, rows)
            h_c, h_lx, h_ux = in_tile(h, j, rows)
            v_c = v[j, rows]
            s_lx, s_ux = 0.5 * (u_lx + u_c), 0.5 * (u_c + u_ux)
            s_ly, s_uy = 0.5 * (v[j, under] + v_c), 0.5 * (v_c + v[j, over])
            flux_lx = jnp.maximum(s_lx, 0.0) * h_lx + jnp.minimum(s_lx, 0.0) * h_c
            flux_ux = jnp.maximum(s_ux, 0.0) * h_c + jnp.minimum(s_ux, 0.0) * h_ux
            flux_ly = jnp.maximum(s_ly, 0.0) * h[j, under] + jnp.minimum(s_ly, 0.0) * h_c
            flux_uy = jnp.maximum(s_uy, 0.0) * h_c + jnp.minimum(s_uy, 0.0) * h[j, over]
            h_next = h_c - TIME_STEP * (flux_ux - flux_lx + flux_uy - flux_ly)
            for k, value in enumerate((u_c, v_c, h_next)):
                results[k, j, start - TOP : start - TOP + part, :] = pltpu.roll(value, back, 1)
        for copy in given(j):
            copy.start()

    for j in range(TPD):
        for copy in given(j):
            copy.wait()


def shards(slots, thickness, driving, friction, velocity_start, row_lengths):
    f32 = jnp.float32
    vmem = pl.BlockSpec(memory_space=pltpu.VMEM)
    smem = pl.BlockSpec(memory_space=pltpu.SMEM)
    anywhere = pl.BlockSpec(memory_space=pl.ANY)
    params = pltpu.CompilerParams(vmem_limit_bytes=VMEM_LIMIT)
    strips_shape = jax.ShapeDtypeStruct((TPD, STRIP, LANES), f32)
    columns_shape = jax.ShapeDtypeStruct((HALF, LANES), f32)
    field_shape = jax.ShapeDtypeStruct((TPD + 1, ROWS, LANES), f32)
    pack_shape = jax.ShapeDtypeStruct((FULL_PACK, LANES), f32)
    rows = row_lengths.shape[0]
    cost = pl.CostEstimate(flops=4_000_000, bytes_accessed=4_000_000, transcendentals=0)
    given = (thickness, driving, friction, velocity_start)

    with jax.named_scope("sent_strips"):
        sent_bottom, sent_top = pl.pallas_call(
            sent_strips_kernel,
            out_shape=(strips_shape, strips_shape),
            in_specs=[anywhere] * 4,
            out_specs=(vmem,) * 2,
            scratch_shapes=[
                pltpu.VMEM((2, 6, TPD, 2 * SECTION, LANES), f32),
                pltpu.SemaphoreType.DMA((2, 6)),
            ],
            compiler_params=pltpu.CompilerParams(vmem_limit_bytes=FIRST_VMEM_LIMIT),
        )(*given)

    with jax.named_scope("own_strips"):
        bottom, top, right, left = pl.pallas_call(
            own_strips_kernel,
            out_shape=(strips_shape, strips_shape, columns_shape, columns_shape),
            in_specs=[vmem] * 4,
            out_specs=(vmem,) * 4,
            cost_estimate=cost,
            compiler_params=params,
        )(*given)

    with jax.named_scope("plan"):
        plan = pl.pallas_call(
            functools.partial(plan_kernel, slots),
            out_shape=jax.ShapeDtypeStruct((1, PLAN), jnp.int32),
            in_specs=[smem],
            out_specs=vmem,
            scratch_shapes=[pltpu.SMEM((1, PLAN), jnp.int32), pltpu.SMEM((rows,), jnp.int32), pltpu.SemaphoreType.DMA],
            cost_estimate=cost,
            compiler_params=params,
        )(row_lengths)

    with jax.named_scope("own_fields"):
        fields = pl.pallas_call(
            own_fields_kernel,
            out_shape=(field_shape,) * 6,
            in_specs=[vmem] * 4,
            out_specs=(vmem,) * 6,
            cost_estimate=cost,
            compiler_params=params,
        )(*given)

    with jax.named_scope("strides"):
        bottoms = [bottom] + [cyclic_shift(sent_bottom, STRIDE * a) for a in range(1, HOPS)]
        tops = [top] + [cyclic_shift(sent_top, -STRIDE * a) for a in range(1, HOPS)]

    with jax.named_scope("route"):
        back, local, ahead = pl.pallas_call(
            route_kernel,
            out_shape=(pack_shape, jax.ShapeDtypeStruct((PACK, LANES), f32), pack_shape),
            in_specs=[vmem] * (2 * HOPS + 3),
            out_specs=(vmem,) * 3,
            scratch_shapes=[pltpu.SMEM((1, PLAN), jnp.int32), pltpu.SemaphoreType.DMA],
            compiler_params=params,
        )(plan, *bottoms, *tops, right, left)

    with jax.named_scope("last_step"):
        back = cyclic_shift(back, -1)
        ahead = cyclic_shift(ahead, 1)

    with jax.named_scope("sweeps"):
        field = pltpu.VMEM(field_shape.shape, f32)
        velocity, thickness_next, *_ = pl.pallas_call(
            sweeps_kernel,
            out_shape=(
                jax.ShapeDtypeStruct(velocity_start.shape, f32),
                jax.ShapeDtypeStruct(thickness.shape, f32),
            ) + (field_shape,) * 6,
            in_specs=[vmem] * 10,
            out_specs=(anywhere, anywhere) + (vmem,) * 6,
            input_output_aliases={4 + k: 2 + k for k in range(6)},
            scratch_shapes=[
                *[field] * 8,
                pltpu.VMEM((3, TPD, TS, LANES), f32),
                pltpu.SemaphoreType.DMA((3, TPD)),
                pltpu.SMEM((1, PLAN), jnp.int32),
                pltpu.SemaphoreType.DMA,
            ],
            compiler_params=params,
        )(plan, ahead, local, back, *fields)
    return velocity, thickness_next


def solution(mesh):
    in_specs = (
        P("ta", None, None),
        P(None, "ta", None, None),
        P(("ma", "ta"), None, None),
        P(None, "ta", None, None),
        P(),
    )
    out_specs = (P(None, ("ma", "ta"), None, None), P(("ma", "ta"), None, None))
    slots = TPD * mesh.shape["ta"]
    return jax.shard_map(
        functools.partial(shards, slots), mesh=mesh, in_specs=in_specs, out_specs=out_specs, check_vma=False
    )
```

```python
import functools

import jax
import jax.numpy as jnp
from jax import lax
from jax.experimental import pallas as pl
from jax.experimental.pallas import tpu as pltpu
from jax.sharding import PartitionSpec as P


GC = 48
SWEEPS = 4
STRAIN_EPSILON = 0.01
TIME_STEP = 0.1

TS = 128
LANES = 128
TPD = 4
SECTION = 8
STRIP = 6 * SECTION
TOP = 16
ROWS = TS + 2 * TOP
MARGIN = 16
STRIDE = 3
HOPS = 5
MAIN_BLOCKS = 2 * TPD
PACK = (MAIN_BLOCKS + 1) * STRIP
CORNER = 8
GROUP = 10
HALF = TS // 2
FULL_PACK = PACK + HALF
VMEM_LIMIT = 40 * 1024 * 1024
FIRST_VMEM_LIMIT = 60 * 1024 * 1024
ROUTE = 3 * TPD * 2 * 3
WHICH = ROUTE
BITS = WHICH + 2 * TPD
PLAN = 128


def cyclic_shift(value, steps):
    count = lax.axis_size("ta")
    return lax.ppermute(value, "ta", [(i, (i + steps) % count) for i in range(count)])


def fill_row_ends(len_ref, ends_ref):
    total = jnp.int32(0)
    ends = []
    for r in range(len_ref.shape[0]):
        total = total + len_ref[r]
        ends_ref[r] = total
        ends.append(total)
    return ends


class Tile:
    def __init__(self, len_ref, ends_ref, ends, slot, slots):
        rows = len_ref.shape[0]
        row = jnp.int32(0)
        for end in ends:
            row = row + jnp.where(end <= slot, 1, 0)
        self.slot = slot
        self.real = (slot >= 0) & (slot < slots)
        row = jnp.minimum(row, rows - 1)
        self.length = len_ref[row]
        self.above = jnp.where(row >= 1, len_ref[jnp.maximum(row - 1, 0)], 0)
        self.below = jnp.where(row < rows - 1, len_ref[jnp.minimum(row + 1, rows - 1)], 0)
        self.column = GC + slot - ends_ref[row]

    def side(self, down, step):
        column = self.column + step
        length = self.below if down else self.above
        there = self.real & (column < GC) & (column >= GC - length)
        slot = self.slot + (self.below if down else -self.length) + step
        return there, slot

    def lower_x(self):
        return self.real & (self.column > GC - self.length)

    def upper_x(self):
        return self.real & (self.column < GC - 1)


def hop(device, slot, down):
    owner = slot >> 2
    q = jnp.maximum((owner - device) if down else (device - owner), 0)
    a = jnp.minimum(((q + 1) * 11) >> 5, HOPS - 1)
    b = q - STRIDE * a
    return a, (-b if down else b)


def field_refs(h_ref, d_ref, f_ref, v_ref):
    return [v_ref.at[0], v_ref.at[1], h_ref, d_ref.at[0], d_ref.at[1], f_ref]


def put_strips(ends, bottom_ref, top_ref):
    row = lax.broadcasted_iota(jnp.int32, (SECTION, LANES), 0)
    for t in range(TPD):
        for k in range(6):
            last = ends(k, t, slice(TS - SECTION, TS))
            first = ends(k, t, slice(0, SECTION))
            if k in (3, 4):
                last = jnp.where(row == 0, ends(k - 3, t, slice(TS - SECTION - 1, TS - SECTION)), last)
                first = jnp.where(row == SECTION - 1, ends(k - 3, t, slice(SECTION, SECTION + 1)), first)
            bottom_ref[t, k * SECTION : (k + 1) * SECTION, :] = last
            top_ref[t, k * SECTION : (k + 1) * SECTION, :] = first


def sent_strips_kernel(h_ref, d_ref, f_ref, v_ref, bottom_ref, top_ref, held, made, sems, out_sems):
    starts = (TS - 2 * SECTION, 0)
    fields = field_refs(h_ref, d_ref, f_ref, v_ref)
    copies = [
        [
            pltpu.make_async_copy(ref.at[:, pl.ds(start, 2 * SECTION)], held.at[side, k], sems.at[side, k])
            for k, ref in enumerate(fields)
        ]
        for side, start in enumerate(starts)
    ]
    for copy in copies[0] + copies[1]:
        copy.start()
    row = lax.broadcasted_iota(jnp.int32, (SECTION, LANES), 0)
    results = [pltpu.make_async_copy(made.at[s], ref, out_sems.at[s]) for s, ref in enumerate((bottom_ref, top_ref))]
    for side in (0, 1):
        for copy in copies[side]:
            copy.wait()
        own = slice(0, SECTION) if side else slice(SECTION, 2 * SECTION)
        ninth = SECTION if side else SECTION - 1
        for t in range(TPD):
            for k in range(6):
                part = held[side, k, t, own, :]
                if k in (3, 4):
                    deepest = row == (SECTION - 1 if side else 0)
                    part = jnp.where(deepest, held[side, k - 3, t, ninth : ninth + 1, :], part)
                made[side, t, k * SECTION : (k + 1) * SECTION, :] = part
        results[side].start()
    for copy in results:
        copy.wait()


def own_strips_kernel(h_ref, d_ref, f_ref, v_ref, bottom_ref, top_ref, right_ref, left_ref):
    fields = field_refs(h_ref, d_ref, f_ref, v_ref)
    put_strips(lambda k, t, rows: fields[k][t, rows, :], bottom_ref, top_ref)
    lane = lax.broadcasted_iota(jnp.int32, (HALF, LANES), 1)
    right = left = jnp.zeros((HALF, LANES), jnp.float32)
    for k, field in enumerate(fields):
        for half in (0, 1):
            start = half * HALF + k * GROUP
            here = (lane >= start) & (lane < start + GROUP)
            rows = slice(half * HALF, (half + 1) * HALF)
            right = jnp.where(here, pltpu.roll(field[TPD - 1, rows, :], (start + GROUP) % LANES, 1), right)
            left = jnp.where(here, pltpu.roll(field[0, rows, :], start, 1) if start else field[0, rows, :], left)
    right_ref[...] = right
    left_ref[...] = left


def plan_kernel(slots, len_ref, out_ref, plan_ref, ends_ref, sem):
    ends = fill_row_ends(len_ref, ends_ref)
    me, count = lax.axis_index("ta"), slots // TPD
    for step in (-1, 0, 1):
        device = lax.rem(me + step + count, count)
        tiles = [Tile(len_ref, ends_ref, ends, device * TPD + j, slots) for j in range(TPD)]
        for j, tile in enumerate(tiles):
            for down in (0, 1):
                for across in (-1, 0, 1):
                    there, slot = tile.side(down, across)
                    a, shift = hop(device, slot, down)
                    entry = (((step + 1) * TPD + j) * 2 + down) * 3 + across + 1
                    plan_ref[0, entry] = jnp.where(there & (shift == step), TPD * a + (slot & 3), -1)
                    if step == 0 and across == 0:
                        plan_ref[0, WHICH + down * TPD + j] = jnp.where(there, shift + 1, -1)
        if step == 0:
            for down in (0, 1):
                plan_ref[0, BITS + down] = flag_bits([t.side(down, k)[0] for t in tiles for k in (-1, 1)])
            plan_ref[0, BITS + 2] = flag_bits([flag for t in tiles for flag in (t.lower_x(), t.upper_x())])
    for unused in range(BITS + 3, PLAN):
        plan_ref[0, unused] = 0
    copy = pltpu.make_async_copy(plan_ref, out_ref, sem)
    copy.start()
    copy.wait()


def flag_bits(flags):
    bits = jnp.int32(0)
    for k, flag in enumerate(flags):
        bits = bits + jnp.where(flag, 1 << k, 0)
    return bits


def own_fields_kernel(h_ref, d_ref, f_ref, v_ref, *outs):
    group = lax.broadcasted_iota(jnp.int32, (TS, LANES), 1) >> 4
    middle = slice(TOP, TOP + TS)
    for ref, out in zip(field_refs(h_ref, d_ref, f_ref, v_ref), outs):
        edges = None
        for j in range(TPD):
            tile = pltpu.roll(ref[j], 2 * MARGIN * j + MARGIN, 1)
            out[j, middle, :] = tile
            edges = tile if j == 0 else jnp.where((group >> 1) == j, tile, edges)
        lower, upper = pltpu.roll(edges, 2 * MARGIN, 1), pltpu.roll(edges, LANES - 2 * MARGIN, 1)
        out[TPD, middle, :] = jnp.where((group & 1) == 0, lower, upper)


def route_kernel(given_plan, *refs):
    given = refs[: 2 * HOPS]
    right_ref, left_ref = refs[2 * HOPS : 2 * HOPS + 2]
    outs = refs[2 * HOPS + 2 : 2 * HOPS + 5]
    plan_ref, sem = refs[2 * HOPS + 5 :]
    copy = pltpu.make_async_copy(given_plan, plan_ref, sem)
    copy.start()
    outs[0][PACK:, :] = left_ref[...]
    outs[2][PACK:, :] = right_ref[...]
    for out in outs:
        out[MAIN_BLOCKS * STRIP : PACK, :] = jnp.zeros((STRIP, LANES), jnp.float32)
    lane = lax.broadcasted_iota(jnp.int32, (STRIP, LANES), 1)
    copy.wait()
    for step, out in enumerate(outs):
        for down in (0, 1):
            for across in (-1, 0, 1):

                @pl.loop(0, TPD)
                def _(j, step=step, out=out, down=down, across=across):
                    source = plan_ref[0, ((step * TPD + j) * 2 + down) * 3 + across + 1]

                    @pl.when(source >= 0)
                    def _():
                        for a in range(HOPS):

                            @pl.when((source >> 2) == a)
                            def _():
                                strip = given[down * HOPS + a][source & 3]
                                turn = 2 * MARGIN * j + MARGIN + (MARGIN * down if across else 0)
                                moved = pltpu.roll(strip, turn & (LANES - 1), 1)
                                if across == 0:
                                    out[pl.ds(pl.multiple_of((down * TPD + j) * STRIP, 8), STRIP), :] = moved
                                else:
                                    rows = slice(MAIN_BLOCKS * STRIP, PACK)
                                    here = (lane >> 3) == ((4 * j + 1 + (across + 1) // 2 + 2 * down) & 15)
                                    out[rows, :] = jnp.where(here, moved, out[rows, :])


def group_mask(bits, shape):
    group = lax.broadcasted_iota(jnp.int32, shape, 1) >> 4
    return ((jnp.full(shape, bits) >> group) & 1) == 1


def sweeps_kernel(given_plan, ahead_ref, local_ref, back_ref, *refs):
    vel_ref, next_ref, u, v, h, d0, d1, f = refs[6:14]
    u_other, v_other, w, ice, u_low, u_high, v_low, v_high, results, out_sems, plan_ref, sem = refs[14:]
    plan_copy = pltpu.make_async_copy(given_plan, plan_ref, sem)
    plan_copy.start()
    packs = (back_ref, local_ref, ahead_ref)
    zero = jnp.zeros((SECTION, LANES), jnp.float32)
    one = jnp.ones((SECTION, LANES), jnp.float32)
    for block in range(TPD + 1):
        for start in (0, ROWS - SECTION):
            rows = slice(start, start + SECTION)
            u[block, rows, :] = zero
            v[block, rows, :] = zero
            w[block, rows, :] = zero
    for j in range(TPD):
        ice[j, TOP : TOP + TS, :] = jnp.ones((TS, LANES), jnp.float32)
    plan_copy.wait()

    targets = (u, v, h, d0, d1, f)
    for down in (0, 1):
        start = TOP + TS if down else TOP - SECTION
        rows = slice(start, start + SECTION)
        deep = SECTION - 1 if down else 0
        far = start + SECTION if down else start - 1

        def put(j, parts, mask=None, rows=rows, deep=deep, far=far):
            for k, target in enumerate(targets):
                target[j, rows, :] = parts[k] if mask is None else jnp.where(mask, parts[k], one if k == 5 else zero)
            for k in (0, 1):
                line = parts[3 + k] if mask is None else jnp.where(mask, parts[3 + k], zero)
                targets[k][j, far : far + 1, :] = line[deep : deep + 1, :]

        def sections(pack, block):
            return [pack[block * STRIP + k * SECTION : block * STRIP + (k + 1) * SECTION, :] for k in range(6)]

        for j in range(TPD):
            which = plan_ref[0, WHICH + down * TPD + j]
            for index, pack in enumerate(packs):

                @pl.when(which == index)
                def _(j=j, pack=pack, down=down, put=put, sections=sections, rows=rows):
                    put(j, sections(pack, down * TPD + j))
                    ice[j, rows, :] = one

            @pl.when(which < 0)
            def _(j=j, put=put, rows=rows):
                put(j, [zero] * 5 + [one])
                ice[j, rows, :] = zero

        within = lax.broadcasted_iota(jnp.int32, (SECTION, LANES), 1) & (2 * MARGIN - 1)
        near = (within >= MARGIN - CORNER) & (within < MARGIN + CORNER)
        mask = group_mask(plan_ref[0, BITS + down], (SECTION, LANES)) & near
        parts = [sum(part) for part in zip(*[sections(pack, MAIN_BLOCKS) for pack in packs])]
        parts = [pltpu.roll(part, LANES - MARGIN, 1) for part in parts] if down else parts
        put(TPD, parts, mask)
        ice[TPD, rows, :] = jnp.where(mask, one, zero)

    mask = group_mask(plan_ref[0, BITS + 2], (TS, LANES))
    group = lax.broadcasted_iota(jnp.int32, (TS, LANES), 1) >> 4
    middle = slice(TOP, TOP + TS)
    ice[TPD, middle, :] = jnp.where(mask, 1.0, 0.0)
    group = group[:HALF]
    for k, target in enumerate(targets):
        for half in (0, 1):
            start = half * HALF + k * GROUP
            rows = slice(TOP + half * HALF, TOP + (half + 1) * HALF)
            before = pltpu.roll(ahead_ref[PACK:, :], (MARGIN - GROUP - start) % LANES, 1)
            after = pltpu.roll(back_ref[PACK:, :], (LANES - MARGIN - start) % LANES, 1)
            beside = jnp.where(group == 0, before, target[TPD, rows, :])
            beside = jnp.where(group == 2 * TPD - 1, after, beside)
            target[TPD, rows, :] = jnp.where(mask[:HALF], beside, 1.0 if k == 5 else 0.0)

    chunk = 24
    first_row, last_row = TOP - SECTION, TOP + TS + SECTION

    def in_tile(ref, j, rows):
        centre, edge = ref[j, rows], ref[TPD, rows]
        lane = lax.broadcasted_iota(jnp.int32, centre.shape, 1)
        high_side = 2 * MARGIN * j + MARGIN
        lower = pltpu.roll(jnp.where(lane == high_side - 1, edge, centre), 1, 1)
        upper = pltpu.roll(jnp.where(lane == high_side, edge, centre), LANES - 1, 1)
        return centre, lower, upper

    def in_columns(ref, j, rows):
        centre, edge = ref[TPD, rows], ref[0, rows]
        lane = lax.broadcasted_iota(jnp.int32, centre.shape, 1)
        for t in range(1, TPD):
            edge = jnp.where((lane >> 5) == t, ref[t, rows], edge)
        within = lane & (2 * MARGIN - 1)
        lower = pltpu.roll(jnp.where(within == MARGIN - 1, edge, centre), 1, 1)
        upper = pltpu.roll(jnp.where(within == MARGIN, edge, centre), LANES - 1, 1)
        return centre, lower, upper

    def viscosity(u, v, j, beside):
        for start in range(first_row, last_row, chunk):
            rows, under, over = (slice(start + k, start + k + chunk) for k in (0, -1, 1))
            _, u_lx, u_ux = beside(u, j, rows)
            _, v_lx, v_ux = beside(v, j, rows)
            u_low[j, rows], u_high[j, rows] = u_lx, u_ux
            v_low[j, rows], v_high[j, rows] = v_lx, v_ux
            ux = u_ux - u_lx
            vy = v[j, over] - v[j, under]
            shear = (u[j, over] - u[j, under]) + (v_ux - v_lx)
            strain = 0.25 * (ux * ux + vy * vy + ux * vy + 0.25 * shear * shear) + STRAIN_EPSILON
            w[j, rows] = (0.25 * h[j, rows]) * jnp.exp(jnp.log(strain) * (-1.0 / 3.0))

    def quotient(top, bottom):
        guess = pl.reciprocal(bottom, approx=True)
        return top * (guess * (2.0 - bottom * guess))

    def relax(u, v, u_next, v_next, j, beside):
        for start in range(first_row, last_row, chunk):
            rows, under, over = (slice(start + k, start + k + chunk) for k in (0, -1, 1))
            here, w_lx, w_ux = beside(w, j, rows)
            c_lx, c_ux = here + w_lx, here + w_ux
            c_ly, c_uy = here + w[j, under], here + w[j, over]
            u_lx, u_ux = u_low[j, rows], u_high[j, rows]
            v_lx, v_ux = v_low[j, rows], v_high[j, rows]
            c_x, c_y = c_lx + c_ux, c_ly + c_uy
            drag = f[j, rows]
            u_top = 4.0 * (c_lx * u_lx + c_ux * u_ux) + c_ly * u[j, under] + c_uy * u[j, over] - d0[j, rows]
            v_top = c_lx * v_lx + c_ux * v_ux + 4.0 * (c_ly * v[j, under] + c_uy * v[j, over]) - d1[j, rows]
            u_new = quotient(u_top, 4.0 * c_x + c_y + drag)
            v_new = quotient(v_top, c_x + 4.0 * c_y + drag)
            if beside is in_columns or start == first_row or start + chunk == last_row:
                is_ice = ice[j, rows] > 0.0
                u_new = jnp.where(is_ice, u_new, 0.0)
                v_new = jnp.where(is_ice, v_new, 0.0)
            u_next[j, rows] = u_new
            v_next[j, rows] = v_new

    def sweep(*state):
        @pl.loop(0, TPD)
        def _(j):
            viscosity(*state[:2], j, in_tile)

        viscosity(*state[:2], TPD, in_columns)

        @pl.loop(0, TPD)
        def _(j):
            relax(*state, j, in_tile)

        relax(*state, TPD, in_columns)

    @pl.loop(0, SWEEPS // 2)
    def _(_):
        sweep(u, v, u_other, v_other)
        sweep(u_other, v_other, u, v)

    def given(j):
        refs = (vel_ref.at[0, j], vel_ref.at[1, j], next_ref.at[j])
        return [pltpu.make_async_copy(results.at[k, j], ref, out_sems.at[k, j]) for k, ref in enumerate(refs)]

    @pl.loop(0, TPD)
    def _(j):
        part = 64
        back = LANES - MARGIN - 2 * MARGIN * j

        for start in range(TOP, TOP + TS, part):
            rows, under, over = (slice(start + k, start + k + part) for k in (0, -1, 1))
            u_c, u_lx, u_ux = in_tile(u, j, rows)
            h_c, h_lx, h_ux = in_tile(h, j, rows)
            v_c = v[j, rows]
            s_lx, s_ux = 0.5 * (u_lx + u_c), 0.5 * (u_c + u_ux)
            s_ly, s_uy = 0.5 * (v[j, under] + v_c), 0.5 * (v_c + v[j, over])
            flux_lx = jnp.maximum(s_lx, 0.0) * h_lx + jnp.minimum(s_lx, 0.0) * h_c
            flux_ux = jnp.maximum(s_ux, 0.0) * h_c + jnp.minimum(s_ux, 0.0) * h_ux
            flux_ly = jnp.maximum(s_ly, 0.0) * h[j, under] + jnp.minimum(s_ly, 0.0) * h_c
            flux_uy = jnp.maximum(s_uy, 0.0) * h_c + jnp.minimum(s_uy, 0.0) * h[j, over]
            h_next = h_c - TIME_STEP * (flux_ux - flux_lx + flux_uy - flux_ly)
            for k, value in enumerate((u_c, v_c, h_next)):
                results[k, j, start - TOP : start - TOP + part, :] = pltpu.roll(value, back, 1)
        for copy in given(j):
            copy.start()

    for j in range(TPD):
        for copy in given(j):
            copy.wait()


def shards(slots, thickness, driving, friction, velocity_start, row_lengths):
    f32 = jnp.float32
    vmem = pl.BlockSpec(memory_space=pltpu.VMEM)
    smem = pl.BlockSpec(memory_space=pltpu.SMEM)
    anywhere = pl.BlockSpec(memory_space=pl.ANY)
    params = pltpu.CompilerParams(vmem_limit_bytes=VMEM_LIMIT)
    strips_shape = jax.ShapeDtypeStruct((TPD, STRIP, LANES), f32)
    columns_shape = jax.ShapeDtypeStruct((HALF, LANES), f32)
    field_shape = jax.ShapeDtypeStruct((TPD + 1, ROWS, LANES), f32)
    pack_shape = jax.ShapeDtypeStruct((FULL_PACK, LANES), f32)
    rows = row_lengths.shape[0]
    cost = pl.CostEstimate(flops=4_000_000, bytes_accessed=4_000_000, transcendentals=0)
    given = (thickness, driving, friction, velocity_start)

    with jax.named_scope("sent_strips"):
        sent_bottom, sent_top = pl.pallas_call(
            sent_strips_kernel,
            out_shape=(strips_shape, strips_shape),
            in_specs=[anywhere] * 4,
            out_specs=(anywhere,) * 2,
            scratch_shapes=[
                pltpu.VMEM((2, 6, TPD, 2 * SECTION, LANES), f32),
                pltpu.VMEM((2, TPD, STRIP, LANES), f32),
                pltpu.SemaphoreType.DMA((2, 6)),
                pltpu.SemaphoreType.DMA((2,)),
            ],
            compiler_params=pltpu.CompilerParams(vmem_limit_bytes=FIRST_VMEM_LIMIT),
        )(*given)

    with jax.named_scope("own_strips"):
        bottom, top, right, left = pl.pallas_call(
            own_strips_kernel,
            out_shape=(strips_shape, strips_shape, columns_shape, columns_shape),
            in_specs=[vmem] * 4,
            out_specs=(vmem,) * 4,
            cost_estimate=cost,
            compiler_params=params,
        )(*given)

    with jax.named_scope("plan"):
        plan = pl.pallas_call(
            functools.partial(plan_kernel, slots),
            out_shape=jax.ShapeDtypeStruct((1, PLAN), jnp.int32),
            in_specs=[smem],
            out_specs=vmem,
            scratch_shapes=[pltpu.SMEM((1, PLAN), jnp.int32), pltpu.SMEM((rows,), jnp.int32), pltpu.SemaphoreType.DMA],
            cost_estimate=cost,
            compiler_params=params,
        )(row_lengths)

    with jax.named_scope("own_fields"):
        fields = pl.pallas_call(
            own_fields_kernel,
            out_shape=(field_shape,) * 6,
            in_specs=[vmem] * 4,
            out_specs=(vmem,) * 6,
            cost_estimate=cost,
            compiler_params=params,
        )(*given)

    with jax.named_scope("strides"):
        bottoms = [bottom] + [cyclic_shift(sent_bottom, STRIDE * a) for a in range(1, HOPS)]
        tops = [top] + [cyclic_shift(sent_top, -STRIDE * a) for a in range(1, HOPS)]

    with jax.named_scope("route"):
        back, local, ahead = pl.pallas_call(
            route_kernel,
            out_shape=(pack_shape, jax.ShapeDtypeStruct((PACK, LANES), f32), pack_shape),
            in_specs=[vmem] * (2 * HOPS + 3),
            out_specs=(vmem,) * 3,
            scratch_shapes=[pltpu.SMEM((1, PLAN), jnp.int32), pltpu.SemaphoreType.DMA],
            compiler_params=params,
        )(plan, *bottoms, *tops, right, left)

    with jax.named_scope("last_step"):
        back = cyclic_shift(back, -1)
        ahead = cyclic_shift(ahead, 1)

    with jax.named_scope("sweeps"):
        field = pltpu.VMEM(field_shape.shape, f32)
        velocity, thickness_next, *_ = pl.pallas_call(
            sweeps_kernel,
            out_shape=(
                jax.ShapeDtypeStruct(velocity_start.shape, f32),
                jax.ShapeDtypeStruct(thickness.shape, f32),
            ) + (field_shape,) * 6,
            in_specs=[vmem] * 10,
            out_specs=(anywhere, anywhere) + (vmem,) * 6,
            input_output_aliases={4 + k: 2 + k for k in range(6)},
            scratch_shapes=[
                *[field] * 8,
                pltpu.VMEM((3, TPD, TS, LANES), f32),
                pltpu.SemaphoreType.DMA((3, TPD)),
                pltpu.SMEM((1, PLAN), jnp.int32),
                pltpu.SemaphoreType.DMA,
            ],
            compiler_params=params,
        )(plan, ahead, local, back, *fields)
    return velocity, thickness_next


def solution(mesh):
    in_specs = (
        P("ta", None, None),
        P(None, "ta", None, None),
        P(("ma", "ta"), None, None),
        P(None, "ta", None, None),
        P(),
    )
    out_specs = (P(None, ("ma", "ta"), None, None), P(("ma", "ta"), None, None))
    slots = TPD * mesh.shape["ta"]
    return jax.shard_map(
        functools.partial(shards, slots), mesh=mesh, in_specs=in_specs, out_specs=out_specs, check_vma=False
    )
```
